128 devices in a mesh: seq: 8 (over y, core), head: 16 (over x, z).
Axes of the slice: x: 4, y: 4, z: 4, core: 2. Of those that a mesh axis runs over, the one named last changes fastest.
Arguments:
- light_query: bfloat16 [8192, 8192], P(('seq', 'head')), may hold values from -6 to 6
- light_key: bfloat16 [8192, 8192], P(('seq', 'head')), may hold values from -6 to 6
- light_value: bfloat16 [8192, 8192], P(('seq', 'head')), may hold values from -12 to 12
- light_decay: bfloat16 [8192, 64], P(('seq', 'head')), may hold values from -1 to 0, as said below
- light_gain: bfloat16 [8192], P('head'), may hold values from 0.5 to 1.5
- soft_query: bfloat16 [8192, 8192], P(('seq', 'head')), may hold values from -6 to 6
- soft_kv: bfloat16 [8192, 2, 1024], P(('seq', 'head')), may hold values from -6 to 6
- doc_blocks: int32 [8], replicated, may hold values from 1 to 32, 64 in all
Outputs:
- light_out: bfloat16 [8192, 8192], P(('seq', 'head'))
- soft_out: bfloat16 [8192, 8192], P(('seq', 'head'))
The draws below stay inside these ranges and needn't reach their ends.
Inputs may be any that keep to these rules, and one draw needn't show every extreme that they name: `doc_blocks`: 8 lengths summing to 64; the longest is exactly 32. `light_decay`: never positive.
All inputs are finite; a program needn't handle non-finite values.
Results may differ from the reference program's by a relative error of at most 0.0085.
Values may be sent and summed in bfloat16 or wider, within the bound.
A program may use at most 128 MiB of HBM per device.

```python
import math
import jax
import jax.numpy as jnp
import numpy as np
from jax import lax

HD = 128
GROUP = 8
BLOCK = 256
QUERY_HEAD_COUNT = 64
KVH = 8
PACKED_TOKENS = 8192
MOST_BLOCKS = 32
DOCS = 8


def draw_soft_query(key, part):
    key = jax.random.fold_in(key, 21)
    drawn = jnp.clip(jax.random.normal(key, (PACKED_TOKENS, QUERY_HEAD_COUNT * HD), jnp.float32), -6.0, 6.0)
    return drawn.astype(jnp.bfloat16)


def draw_soft_kv(key, part):
    key = jax.random.fold_in(key, 22)
    drawn = jnp.clip(jax.random.normal(key, (PACKED_TOKENS, 2, KVH * HD), jnp.float32), -6.0, 6.0)
    return drawn.astype(jnp.bfloat16)


def draw_light_decay(key, part):
    key = jax.random.fold_in(key, 31)
    random_subkeys = jax.random.split(key, 6)
    longest = MOST_BLOCKS * 128.0
    slow_share = 0.5
    slow_head = jax.random.uniform(random_subkeys[0], (QUERY_HEAD_COUNT,)) < slow_share
    slow_rate = jnp.exp(jax.random.uniform(random_subkeys[1], (QUERY_HEAD_COUNT,), jnp.float32, math.log(0.03), math.log(0.3))) / longest
    fast_rate = jnp.exp(jax.random.uniform(random_subkeys[2], (QUERY_HEAD_COUNT,), jnp.float32, math.log(1.0 / 50.0), math.log(1.0 / 30.0)))
    per_head_rate = jnp.where(slow_head, slow_rate, fast_rate)
    position_weighting = jax.random.uniform(random_subkeys[3], (PACKED_TOKENS, QUERY_HEAD_COUNT), jnp.float32, 0.5, 1.5)
    segment_rows = jax.random.randint(random_subkeys[4], (4,), 0, PACKED_TOKENS)
    segment_mask = jnp.any(jnp.arange(PACKED_TOKENS)[:, None] == segment_rows[None, :], axis=1)
    segment_dropped = jnp.log(jax.random.uniform(random_subkeys[5], (PACKED_TOKENS, QUERY_HEAD_COUNT), jnp.float32, 0.55, 0.8))
    decay_amount = -per_head_rate[None, :] * position_weighting + jnp.where(segment_mask[:, None], segment_dropped, 0.0)
    return decay_amount.astype(jnp.bfloat16)


def draw_light_value(key, part):
    key = jax.random.fold_in(key, 41)
    key_scale, key_base = jax.random.split(key)
    columns = jnp.exp(jax.random.uniform(key_scale, (QUERY_HEAD_COUNT * HD,), jnp.float32, math.log(0.3), math.log(3.0)))
    drawn = jnp.clip(jax.random.normal(key_base, (PACKED_TOKENS, QUERY_HEAD_COUNT * HD), jnp.float32), -4.0, 4.0)
    return (drawn * columns[None, :]).astype(jnp.bfloat16)


def levels(key, shape, shards, low, top_value):
    factor_of, own = 1.0, jax.random.fold_in(key, 6)
    for dim, shards_of in shards:
        heights = jnp.exp(jax.random.uniform(jax.random.fold_in(own, dim), (shards_of,), jnp.float32, low / len(shards), top_value / len(shards)))
        factor_of = factor_of * jnp.repeat(heights, shape[dim] // shards_of).reshape([-1 if axis == dim else 1 for axis in range(len(shape))])
    return factor_of


def split_up(amount, total, most, skew):
    portions = [(1 << 20) // math.isqrt(rank ** skew) + 1 for rank in range(2, amount + 1)]
    surplus, counts = total - most - (amount - 1), [1] * (amount - 1)
    while surplus > 0:
        free = [i for i in range(amount - 1) if counts[i] < most]
        pool, budget = sum([portions[i] for i in free]), surplus
        for i in free:
            more = min(most - counts[i], max(1, budget * portions[i] // pool), surplus)
            counts[i] = counts[i] + more
            surplus = surplus - more
    return np.array([most] + counts)


def uneven_parts(key, amount, total, bound, lean):
    if amount == 2:
        one = jax.random.randint(key, (), max(1, total - bound), min(bound, total - 1) + 1)
        return jnp.stack([one, total - one])
    tallies = jnp.asarray(split_up(amount, total, bound, lean), jnp.int32)
    twos = (amount - 1) // 2
    donor, sink = tallies[1:1 + 2 * twos:2], tallies[2:2 + 2 * twos:2]
    margin = jnp.minimum(donor - 1, bound - sink)
    passed = jax.random.randint(jax.random.fold_in(key, 1), (twos,), 0, 1 << 20) % (margin + 1)
    tallies = tallies.at[1:1 + 2 * twos:2].set(donor - passed).at[2:2 + 2 * twos:2].set(sink + passed)
    return tallies[jax.random.permutation(jax.random.fold_in(key, 2), amount)]


def bell_draw(own_key, extent, width, reach, pieces=(), kind=jnp.bfloat16):
    result = jax.random.normal(own_key, extent, jnp.float32) * width
    if len(pieces) > 0:
        result = levels(own_key, extent, pieces, -0.22, 0.18) * result
    return jnp.clip(result, min=-reach, max=reach).astype(kind)


def setup_inputs(seed: int = 0) -> dict:
    keys = jax.random.split(jax.random.key(seed), 9)
    return {
        "light_query": bell_draw(keys[0], (PACKED_TOKENS, QUERY_HEAD_COUNT * HD), 1.0, 6.0, ((0, 128),)),
        "light_key": bell_draw(keys[1], (PACKED_TOKENS, QUERY_HEAD_COUNT * HD), 1.0, 6.0, ((0, 128),)),
        "light_value": draw_light_value(jax.random.fold_in(keys[8], 71), 0),
        "light_decay": draw_light_decay(jax.random.fold_in(keys[8], 71), 0),
        "light_gain": jnp.clip(1.0 + 0.1 * jax.random.normal(keys[4], (QUERY_HEAD_COUNT * HD,), jnp.float32), 0.5, 1.5).astype(jnp.bfloat16),
        "soft_query": draw_soft_query(jax.random.fold_in(keys[8], 71), 0),
        "soft_kv": draw_soft_kv(jax.random.fold_in(keys[8], 71), 0),
        "doc_blocks": uneven_parts(keys[7], DOCS, PACKED_TOKENS // 128, MOST_BLOCKS, 2).astype(jnp.int32),
    }


highest = lax.Precision.HIGHEST
eps_norm = 1e-06

def doc_index(positions, doc_blocks):
    doc_ends = (jnp.cumsum(doc_blocks) * 128).astype(jnp.int32)
    return lax.optimization_barrier(jnp.sum((positions[:, None] >= doc_ends[None, :]).astype(jnp.int32), axis=1)).astype(jnp.int32)

def lightning_scan(query_rows, key_rows, value_rows, decay_rows, doc_ids, prior_doc, head_state):
    length = query_rows.shape[0]
    row_order = jnp.arange(BLOCK)
    causal = row_order[:, None] >= row_order[None, :]

    def one_block(state_carry, block_index):
        block_state, block_prior = state_carry
        offset = block_index.astype(jnp.int32) * BLOCK
        block_query = lax.dynamic_slice_in_dim(query_rows, offset, BLOCK, 0)
        block_key = lax.dynamic_slice_in_dim(key_rows, offset, BLOCK, 0)
        block_value = lax.dynamic_slice_in_dim(value_rows, offset, BLOCK, 0)
        block_decay = lax.dynamic_slice_in_dim(decay_rows, offset, BLOCK, 0)
        block_docs = lax.dynamic_slice_in_dim(doc_ids, offset, BLOCK, 0)
        cumulative = jnp.cumsum(block_decay, axis=0)
        allowed = (causal & (block_docs[:, None] == block_docs[None, :]))[None]
        decay_gap = cumulative.T[:, :, None] - cumulative.T[:, None, :]
        decay_weight = jnp.where(allowed, jnp.exp(jnp.where(allowed, decay_gap, 0.0)), 0.0)
        scores = jnp.einsum('thd,jhd->htj', block_query, block_key, precision=highest)
        inner_out = jnp.einsum('htj,jhd->thd', scores * decay_weight, block_value, precision=highest)
        carried = (block_docs == block_prior).astype(jnp.float32)
        carried_out = jnp.einsum('thd,hde->the', block_query, block_state, precision=highest) * (jnp.exp(cumulative) * carried[:, None])[:, :, None]
        last_doc = block_docs[BLOCK - 1]
        tail_weight = jnp.exp(cumulative[BLOCK - 1][None, :] - cumulative) * (block_docs == last_doc).astype(jnp.float32)[:, None]
        keep_old = (last_doc == block_prior).astype(jnp.float32)
        new_state = block_state * (jnp.exp(cumulative[BLOCK - 1]) * keep_old)[:, None, None] + jnp.einsum('jhd,jh,jhe->hde', block_key, tail_weight, block_value, precision=highest)
        return ((new_state, last_doc), inner_out + carried_out)
    (final_state, final_doc), outputs = lax.scan(one_block, (head_state, prior_doc), jnp.arange(length // BLOCK))
    return (outputs.reshape(query_rows.shape), final_state)

def head_norm(mixed_rows, light_gain):
    mean_square = lax.optimization_barrier(jnp.mean(mixed_rows * mixed_rows, axis=-1, keepdims=True))
    gain_cols = light_gain.astype(jnp.float32).reshape(1, -1, mixed_rows.shape[-1])
    return (mixed_rows * lax.rsqrt(mean_square + eps_norm) * gain_cols).astype(jnp.bfloat16)

def reference(light_query, light_key, light_value, light_decay, light_gain, soft_query, soft_kv, doc_blocks):
    positions = jnp.arange(PACKED_TOKENS, dtype=jnp.int32)
    doc_ids = doc_index(positions, doc_blocks)
    head_shape = (PACKED_TOKENS, QUERY_HEAD_COUNT, HD)
    mixed_rows, final_state = lightning_scan(light_query.astype(jnp.float32).reshape(head_shape), light_key.astype(jnp.float32).reshape(head_shape), light_value.astype(jnp.float32).reshape(head_shape), light_decay.astype(jnp.float32), doc_ids, jnp.int32(-1), jnp.zeros((QUERY_HEAD_COUNT, HD, HD), jnp.float32))
    light_out = head_norm(mixed_rows, light_gain).reshape(PACKED_TOKENS, QUERY_HEAD_COUNT * HD)
    query_blocks = PACKED_TOKENS // 512
    query_all = soft_query.reshape(PACKED_TOKENS, KVH, GROUP, HD)
    key_all = soft_kv[:, 0, :].reshape(PACKED_TOKENS, KVH, HD)
    value_all = soft_kv[:, 1, :].reshape(PACKED_TOKENS, KVH, HD)
    score_scale = 1.0 / math.sqrt(HD)

    def one_item(item_index):
        kv_head = (item_index // query_blocks).astype(jnp.int32)
        row_start = (item_index % query_blocks * 512).astype(jnp.int32)
        key_head = lax.dynamic_index_in_dim(key_all, kv_head, 1, False).astype(jnp.float32)
        value_head = lax.dynamic_index_in_dim(value_all, kv_head, 1, False).astype(jnp.float32)
        query_head = lax.dynamic_index_in_dim(query_all, kv_head, 1, False)
        query_block = lax.dynamic_slice_in_dim(query_head, row_start, 512, 0).astype(jnp.float32)
        scores = jnp.einsum('tgd,kd->tgk', query_block, key_head, precision=highest) * score_scale
        query_pos = row_start + jnp.arange(512, dtype=jnp.int32)
        query_docs = lax.dynamic_slice_in_dim(doc_ids, row_start, 512, 0)
        allowed = ((query_docs[:, None] == doc_ids[None, :]) & (positions[None, :] <= query_pos[:, None]))[:, None, :]
        row_max = lax.optimization_barrier(jnp.max(jnp.where(allowed, scores, -jnp.inf), axis=-1, keepdims=True))
        weights = jnp.where(allowed, jnp.exp(scores - row_max), 0.0)
        denominator = lax.optimization_barrier(jnp.sum(weights, axis=-1))
        rounded = lax.optimization_barrier(weights.astype(jnp.bfloat16)).astype(jnp.float32)
        numerator = jnp.einsum('tgk,kd->tgd', rounded, value_head, precision=highest)
        return (numerator / denominator[:, :, None]).astype(jnp.bfloat16)
    items = lax.map(one_item, jnp.arange(KVH * query_blocks, dtype=jnp.int32))
    soft_out = items.reshape(KVH, query_blocks, 512, GROUP, HD).transpose(1, 2, 0, 3, 4).reshape(PACKED_TOKENS, QUERY_HEAD_COUNT * HD)
    return (light_out, soft_out)
```

```python
import functools
import math

import jax
import jax.numpy as jnp
from jax import lax
from jax.experimental import pallas as pl
from jax.experimental.pallas import tpu as pltpu
from jax.sharding import PartitionSpec as P

MESH = pl.DeviceIdType.MESH
F32, BF16 = jnp.float32, jnp.bfloat16
HD = 128
RUN = 256
PIECE = 64
WIDE = 1024
SHARD = 1024
SPAN = 1024
LOG2E = math.log2(math.e)
SCALE = LOG2E / math.sqrt(HD)
NEG = -1e30

KV, DEC, GAIN, LK, LV, LQ, SQ, ST, TOT, IN, LO, SO, ZS, XS, KINDS = range(15)

NT = (((1,), (1,)), ((), ()))
TN = (((0,), (0,)), ((), ()))


def kernel(
    docs_ref, lq_ref, lk_ref, lv_ref, dec_ref, gain_ref, sq_ref, kv_ref,
    lo_ref, so_ref,
    lq, lk, lv, dec_out, dec, gains, inner, lout, part, tot, parts, tots, back, incoming,
    sq, kv, sout, cums, send, recv, z_recv, x_recv,
):
    s = lax.axis_index("seq")
    h = lax.axis_index("head")
    y, c = s // 2, s % 2
    x, z = h // 4, h % 4
    group = c * 4 + z
    member = y * 4 + x

    def yc(d):
        return (s + d) % 8

    def zc(d):
        other = (group + d) % 8
        return other, (y * 2 + other // 4, x * 4 + other % 4)

    def xz(d):
        return (s, (h + d) % 16)

    def xy(d):
        other = (member + d) % 16
        return other, ((other // 4) * 2 + c, (other % 4) * 4 + z)

    def push(kind, src, dst, device, recv_sem=None):
        pltpu.make_async_remote_copy(
            src_ref=src, dst_ref=dst, send_sem=send.at[kind],
            recv_sem=recv.at[kind] if recv_sem is None else recv_sem,
            device_id=device, device_id_type=MESH,
        ).start()

    def keep(kind, src, dst):
        pltpu.make_async_copy(src, dst, recv.at[kind]).start()

    def landed(sem, ref):
        pltpu.make_async_copy(ref, ref, sem).wait()

    def each(n, body):
        def step(d, carry):
            body(d)
            return carry
        lax.fori_loop(1, n, step, 0)

    barrier = pltpu.get_barrier_semaphore()

    def greet(device):
        pl.semaphore_signal(barrier, inc=1, device_id=device, device_id_type=MESH)

    each(8, lambda d: greet((yc(d), h)))
    each(8, lambda d: greet(zc(d)[1]))
    each(16, lambda d: greet(xz(d)))
    each(16, lambda d: greet(xy(d)[1]))
    wide = jnp.concatenate([dec_ref[...], dec_ref[...]], axis=1).astype(F32)
    for g in range(8):
        dec_out[g] = (wide if g == 0 else pltpu.roll(wide, 128 - 8 * g, 1)).astype(BF16)
    pl.semaphore_wait(barrier, 7 + 7 + 15 + 15)

    mine = pl.ds(s * SHARD + h * PIECE, PIECE)

    def send_kv(d):
        to = yc(d)
        push(KV, kv_ref.at[:, pl.ds(to * HD, HD)], kv.at[mine, pl.ds(0, HD)], (to, h))
        push(KV, kv_ref.at[:, pl.ds(WIDE + to * HD, HD)], kv.at[mine, pl.ds(HD, HD)], (to, h))

    each(8, send_kv)
    keep(KV, kv_ref.at[:, pl.ds(s * HD, HD)], kv.at[mine, pl.ds(0, HD)])
    keep(KV, kv_ref.at[:, pl.ds(WIDE + s * HD, HD)], kv.at[mine, pl.ds(HD, HD)])

    rows = pl.ds(z * PIECE, PIECE)

    def send_light(kind, ref, buf):
        def one(d):
            other, device = zc(d)
            push(kind, ref.at[:, pl.ds(other * WIDE, WIDE)], buf.at[c, rows, :], device)
        each(8, one)
        keep(kind, ref.at[:, pl.ds(group * WIDE, WIDE)], buf.at[c, rows, :])

    def send_dec(d):
        other, device = zc(d)
        push(DEC, dec_out.at[other], dec.at[c, rows, :], device)

    each(8, send_dec)
    keep(DEC, dec_out.at[group], dec.at[c, rows, :])
    send_light(LK, lk_ref, lk)
    send_light(LV, lv_ref, lv)

    def send_sq(d):
        to = yc(d)
        push(SQ, sq_ref.at[:, pl.ds(to * WIDE, WIDE)], sq.at[s], (to, h))

    each(8, send_sq)
    keep(SQ, sq_ref.at[:, pl.ds(s * WIDE, WIDE)], sq.at[s])

    landed(recv.at[KV], kv.at[pl.ds(0, 8 * PIECE)])

    def send_z(t, carry):
        part_rows = kv.at[pl.ds(t * SHARD + h * PIECE, PIECE)]
        def one(d):
            push(ZS, part_rows, part_rows, (s, x * 4 + (z + d) % 4), z_recv.at[t])
        each(4, one)
        return carry

    lax.fori_loop(0, 8, send_z, 0)
    send_light(LQ, lq_ref, lq)

    def send_gain(d):
        push(GAIN, gain_ref, gains.at[h], xz(d))

    each(16, send_gain)
    keep(GAIN, gain_ref, gains.at[h])

    def send_x(t, carry):
        landed(z_recv.at[t], kv.at[pl.ds(0, 3 * PIECE)])
        part_rows = kv.at[pl.ds(t * SHARD + x * RUN, RUN)]
        def one(d):
            push(XS, part_rows, part_rows, (s, ((x + d) % 4) * 4 + z), x_recv.at[t])
        each(4, one)
        return carry

    lax.fori_loop(0, 8, send_x, 0)

    ends = []
    total = jnp.int32(0)
    for i in range(8):
        total = total + docs_ref[i] * 128
        ends.append(total)

    def doc_of(pos):
        found = jnp.zeros_like(pos)
        for end in ends:
            found = found + jnp.where(pos >= end, 1, 0)
        return found

    column = lax.broadcasted_iota(jnp.int32, (RUN, 1), 0)
    line = lax.broadcasted_iota(jnp.int32, (1, RUN), 1)
    causal = column >= line
    lower = jnp.where(causal, 1.0, 0.0).astype(BF16)

    def run_start(i):
        return (2 * y + i) * SHARD + x * RUN

    landed(recv.at[DEC], dec)
    landed(recv.at[LK], lk)
    landed(recv.at[LV], lv)

    def add_states(i, carry):
        cum = jnp.dot(lower, dec[i], preferred_element_type=F32)
        cums[i] = cum
        start = run_start(i)
        last = doc_of(start + RUN - 1)
        tail = jnp.exp(cum[RUN - 1:RUN, :] - cum) * jnp.where(doc_of(start + column) == last, 1.0, 0.0)
        tot[i] = jnp.broadcast_to(cum.T[0:8, RUN - 1:RUN], (8, 128))
        for j in range(8):
            cols = pl.ds(j * HD, HD)
            weighted = (lv[i, :, cols].astype(F32) * tail[:, j:j + 1]).astype(BF16)
            added = lax.dot_general(lk[i, :, cols], weighted, TN, preferred_element_type=F32)
            part[i, pl.ds(j * HD, HD), :] = added.astype(BF16)
        return carry

    lax.fori_loop(0, 2, add_states, 0)

    def send_state(d):
        other, device = xy(d)
        push(TOT, tot, tots.at[y, :, x], device)
        push(ST, part.at[:, pl.ds(other * 64, 64), :], parts.at[y, :, x], device)

    each(16, send_state)
    keep(TOT, tot, tots.at[y, :, x])
    keep(ST, part.at[:, pl.ds(member * 64, 64), :], parts.at[y, :, x])

    landed(recv.at[LQ], lq)

    def inner_run(i, carry):
        cum = cums[i]
        across = cum.T
        start = run_start(i)
        allowed = causal & (doc_of(start + column) == doc_of(start + line))
        for j in range(8):
            cols = pl.ds(j * HD, HD)
            gap = cum[:, j:j + 1] - across[j:j + 1, :]
            weight = jnp.exp(jnp.where(allowed, gap, NEG))
            scores = lax.dot_general(lq[i, :, cols], lk[i, :, cols], NT, preferred_element_type=F32)
            inner[i, :, cols] = jnp.dot(
                (scores * weight).astype(BF16), lv[i, :, cols], preferred_element_type=F32
            )
        return carry

    lax.fori_loop(0, 2, inner_run, 0)

    landed(recv.at[TOT], tots)
    landed(recv.at[ST], parts)

    def scan_runs(p, state):
        a, b, e = p // 8, (p // 4) % 2, p % 4
        back[a, b, e] = state.astype(BF16)
        start = p * RUN
        same = jnp.where(doc_of(start + RUN - 1) == doc_of(start - 1), 1.0, 0.0)
        factor = jnp.exp(tots[a, b, e, pl.ds(member // 2, 1), :]) * same
        return state * factor + parts[a, b, e].astype(F32)

    lax.fori_loop(0, 32, scan_runs, jnp.zeros((64, HD), F32))

    def send_back(d):
        other, device = xy(d)
        push(IN, back.at[other // 4, :, other % 4], incoming.at[:, pl.ds(member * 64, 64), :], device)

    each(16, send_back)
    keep(IN, back.at[y, :, x], incoming.at[:, pl.ds(member * 64, 64), :])

    landed(recv.at[SQ], sq)
    token = lax.broadcasted_iota(jnp.int32, (8 * PIECE, 1), 0) % PIECE
    key_line = lax.broadcasted_iota(jnp.int32, (1, SPAN), 1)

    def soft_piece(t, carry):
        landed(x_recv.at[t], kv.at[pl.ds(0, 3 * RUN)])
        first = t * SHARD + h * PIECE
        doc_start = jnp.int32(0)
        for end in ends:
            doc_start = jnp.where(first >= end, end, doc_start)
        query = jnp.concatenate([sq[t, :, pl.ds(j * HD, HD)] for j in range(8)], axis=0)

        def block(k, stats, diagonal):
            top, denominator, acc = stats
            limit = first + PIECE - SPAN * k
            start = pl.multiple_of(jnp.maximum(limit - SPAN, 0), PIECE)
            key_pos = start + key_line
            scores = lax.dot_general(
                query, kv[pl.ds(start, SPAN), pl.ds(0, HD)], NT, preferred_element_type=F32
            )
            if diagonal:
                kept = (key_pos >= doc_start) & (key_pos <= first + token)
                scores = jnp.where(kept, scores, NEG)
            else:
                kept = (key_pos >= doc_start) & (key_pos < limit)
                scores = scores + jnp.where(kept, 0.0, NEG)
            new_top = jnp.max(scores, axis=1, keepdims=True)
            if not diagonal:
                new_top = jnp.maximum(top, new_top)
            weights = jnp.exp2((scores - new_top) * SCALE)
            summed = jnp.sum(weights, axis=1, keepdims=True)
            product = jnp.dot(
                weights.astype(BF16), kv[pl.ds(start, SPAN), pl.ds(HD, HD)],
                preferred_element_type=F32,
            )
            if diagonal:
                return new_top, summed, product
            rescale = jnp.exp2((top - new_top) * SCALE)
            return new_top, denominator * rescale + summed, acc * rescale + product

        stats = block(0, (None, None, None), True)
        top, denominator, acc = lax.fori_loop(
            1, jnp.minimum(t + 1, 4), lambda k, st: block(k, st, False), stats
        )
        result = (acc / denominator).astype(BF16)
        for j in range(8):
            sout[t, :, pl.ds(j * HD, HD)] = result[j * PIECE:(j + 1) * PIECE, :]

        target = so_ref.at[:, pl.ds(s * WIDE, WIDE)]

        @pl.when(t == s)
        def _():
            keep(SO, sout.at[t], target)

        @pl.when(t != s)
        def _():
            push(SO, sout.at[t], target, (t, h))
        return carry

    lax.fori_loop(0, 4, soft_piece, 0)

    landed(recv.at[GAIN], gains)
    landed(recv.at[IN], incoming)

    def finish(i, carry):
        start = run_start(i)
        carried = jnp.where(doc_of(start + column) == doc_of(start - 1), 1.0, 0.0)
        reach = jnp.exp(cums[i]) * carried
        for j in range(8):
            cols = pl.ds(j * HD, HD)
            entering = jnp.dot(
                lq[i, :, cols], incoming[i, pl.ds(j * HD, HD), :], preferred_element_type=F32
            )
            mixed = inner[i, :, cols] + entering * reach[:, j:j + 1]
            mean_square = jnp.mean(mixed * mixed, axis=1, keepdims=True)
            gain = gains[2 * group + j // 4, pl.ds(j % 4, 1), :]
            lout[i, :, cols] = (mixed * lax.rsqrt(mean_square + 1e-6) * gain).astype(BF16)
        return carry

    lax.fori_loop(0, 2, finish, 0)

    target = lo_ref.at[:, pl.ds(group * WIDE, WIDE)]

    def send_out(d):
        other, device = zc(d)
        push(LO, lout.at[other // 4, pl.ds((other % 4) * PIECE, PIECE), :], target, device)

    each(8, send_out)
    keep(LO, lout.at[c, rows, :], target)

    lax.fori_loop(4, 8, soft_piece, 0)

    landed(send.at[KV], kv.at[pl.ds(0, 7 * PIECE)])
    landed(send.at[DEC], dec_out.at[pl.ds(0, 7)])
    landed(send.at[GAIN], gains.at[pl.ds(0, 15)])
    for kind in (LK, LV, LQ, SQ, LO, SO):
        landed(send.at[kind], sq.at[pl.ds(0, 7)])
    landed(send.at[ZS], kv.at[pl.ds(0, 24 * PIECE)])
    landed(send.at[XS], kv.at[pl.ds(0, 24 * RUN)])
    landed(send.at[TOT], inner.at[0, pl.ds(0, 15 * 16), pl.ds(0, HD)])
    landed(send.at[ST], kv.at[pl.ds(0, 15 * 64)])
    landed(send.at[IN], kv.at[pl.ds(0, 15 * 64)])
    landed(recv.at[LO], lo_ref)
    landed(recv.at[SO], so_ref)


def per_device(
    light_query, light_key, light_value, light_decay, light_gain, soft_query, soft_kv, doc_blocks
):
    gain = jnp.pad(light_gain.astype(F32).reshape(4, HD), ((0, 4), (0, 0)))
    kv = soft_kv.reshape(PIECE, 2 * WIDE)
    anywhere = pl.BlockSpec(memory_space=pl.ANY)
    vmem = pl.BlockSpec(memory_space=pltpu.VMEM)
    out = jax.ShapeDtypeStruct((PIECE, 8 * WIDE), BF16)
    scratch = [
        pltpu.VMEM((2, RUN, WIDE), BF16),
        pltpu.VMEM((2, RUN, WIDE), BF16),
        pltpu.VMEM((2, RUN, WIDE), BF16),
        pltpu.VMEM((8, PIECE, 128), BF16),
        pltpu.VMEM((2, RUN, 128), BF16),
        pltpu.VMEM((16, 8, HD), F32),
        pltpu.VMEM((2, RUN, WIDE), F32),
        pltpu.VMEM((2, RUN, WIDE), BF16),
        pltpu.VMEM((2, WIDE, HD), BF16),
        pltpu.VMEM((2, 8, 128), F32),
        pltpu.VMEM((4, 2, 4, 64, HD), BF16),
        pltpu.VMEM((4, 2, 4, 8, 128), F32),
        pltpu.VMEM((4, 2, 4, 64, HD), BF16),
        pltpu.VMEM((2, WIDE, HD), BF16),
        pltpu.VMEM((8, PIECE, WIDE), BF16),
        pltpu.VMEM((8 * SHARD, 2 * HD), BF16),
        pltpu.VMEM((8, PIECE, WIDE), BF16),
        pltpu.VMEM((2, RUN, 128), F32),
        pltpu.SemaphoreType.DMA((KINDS,)),
        pltpu.SemaphoreType.DMA((KINDS,)),
        pltpu.SemaphoreType.DMA((8,)),
        pltpu.SemaphoreType.DMA((8,)),
    ]
    return pl.pallas_call(
        kernel,
        out_shape=(out, out),
        in_specs=[
            pl.BlockSpec(memory_space=pltpu.SMEM), anywhere, anywhere, anywhere, vmem, anywhere,
            anywhere, anywhere,
        ],
        out_specs=(anywhere, anywhere),
        scratch_shapes=scratch,
        compiler_params=pltpu.CompilerParams(
            collective_id=0, has_side_effects=True, vmem_limit_bytes=48 * 2**20
        ),
    )(doc_blocks, light_query, light_key, light_value, light_decay, gain, soft_query, kv)


def solution(mesh):
    placed = (
        P(("seq", "head"), None),
        P(("seq", "head"), None),
        P(("seq", "head"), None),
        P(("seq", "head"), None),
        P("head"),
        P(("seq", "head"), None),
        P(("seq", "head"), None, None),
        P(),
    )
    return jax.shard_map(
        per_device,
        mesh=mesh,
        in_specs=placed,
        out_specs=(P(("seq", "head"), None), P(("seq", "head"), None)),
        check_vma=False,
    )
```

```python
import functools
import math

import jax
import jax.numpy as jnp
from jax import lax
from jax.experimental import pallas as pl
from jax.experimental.pallas import tpu as pltpu
from jax.sharding import PartitionSpec as P

MESH = pl.DeviceIdType.MESH
F32, BF16 = jnp.float32, jnp.bfloat16
HD = 128
RUN = 256
PIECE = 64
WIDE = 1024
SHARD = 1024
SPAN = 1024
LOG2E = math.log2(math.e)
SCALE = LOG2E / math.sqrt(HD)
NEG = -1e30

KV, DEC, GAIN, GAINS, SQ, TOT, SO, ZS, XS = range(9)
LK, LV, LQ, ST, IN, LO = ((9 + 2 * i, 10 + 2 * i) for i in range(6))
KINDS = 21
HALF = WIDE // 2
SLICE = 32

NT = (((1,), (1,)), ((), ()))
TN = (((0,), (0,)), ((), ()))


def kernel(
    docs_ref, lq_ref, lk_ref, lv_ref, dec_ref, gain_ref, sq_ref, kv_ref,
    lo_ref, so_ref,
    lq, lk, lv, dec_out, dec, gains, inner, lout, part, tot, parts, tots, back, incoming,
    sq, kv, sout, cums, gain_out, send, recv, z_recv, left_recv, right_recv, far_recv,
):
    s = lax.axis_index("seq")
    h = lax.axis_index("head")
    y, c = s // 2, s % 2
    x, z = h // 4, h % 4
    group = c * 4 + z
    member = y * 4 + x

    def yc(d):
        return (s + d) % 8

    def zc(d):
        other = (group + d) % 8
        return other, (y * 2 + other // 4, x * 4 + other % 4)

    def along_x(d):
        return (s, ((x + d) % 4) * 4 + z)

    def along_z(d):
        return (s, x * 4 + (z + d) % 4)

    def xy(d):
        other = (member + d) % 16
        return other, ((other // 4) * 2 + c, (other % 4) * 4 + z)

    def push(kind, src, dst, device, recv_sem=None):
        pltpu.make_async_remote_copy(
            src_ref=src, dst_ref=dst, send_sem=send.at[kind],
            recv_sem=recv.at[kind] if recv_sem is None else recv_sem,
            device_id=device, device_id_type=MESH,
        ).start()

    def keep(kind, src, dst):
        pltpu.make_async_copy(src, dst, recv.at[kind]).start()

    def landed(sem, ref):
        pltpu.make_async_copy(ref, ref, sem).wait()

    def each(n, body):
        def step(d, carry):
            body(d)
            return carry
        lax.fori_loop(1, n, step, 0)

    barrier = pltpu.get_barrier_semaphore()

    def greet(device):
        pl.semaphore_signal(barrier, inc=1, device_id=device, device_id_type=MESH)

    each(8, lambda d: greet((yc(d), h)))
    each(8, lambda d: greet(zc(d)[1]))
    each(16, lambda d: greet(xy(d)[1]))
    gain = gain_ref[...].astype(F32)
    gain_out[...] = jnp.concatenate([gain, gain], axis=0)
    wide = jnp.concatenate([dec_ref[...], dec_ref[...]], axis=1).astype(F32)
    for g in range(8):
        dec_out[g] = (wide if g == 0 else pltpu.roll(wide, 128 - 8 * g, 1)).astype(BF16)
    pl.semaphore_wait(barrier, 7 + 7 + 15)

    mine = pl.ds(s * SHARD + h * PIECE, PIECE)

    def send_kv(d):
        to = yc(d)
        push(KV, kv_ref.at[:, pl.ds(to * HD, HD)], kv.at[mine, pl.ds(0, HD)], (to, h))
        push(KV, kv_ref.at[:, pl.ds(WIDE + to * HD, HD)], kv.at[mine, pl.ds(HD, HD)], (to, h))

    each(8, send_kv)
    keep(KV, kv_ref.at[:, pl.ds(s * HD, HD)], kv.at[mine, pl.ds(0, HD)])
    keep(KV, kv_ref.at[:, pl.ds(WIDE + s * HD, HD)], kv.at[mine, pl.ds(HD, HD)])

    rows = pl.ds(z * PIECE, PIECE)

    def send_light(kinds, half, ref, buf):
        place = buf.at[c, rows, pl.ds(half * HALF, HALF)]
        def one(d):
            other, device = zc(d)
            push(kinds[half], ref.at[:, pl.ds(other * WIDE + half * HALF, HALF)], place, device)
        each(8, one)
        keep(kinds[half], ref.at[:, pl.ds(group * WIDE + half * HALF, HALF)], place)

    def send_dec(d):
        other, device = zc(d)
        push(DEC, dec_out.at[other], dec.at[c, rows, :], device)

    each(8, send_dec)
    keep(DEC, dec_out.at[group], dec.at[c, rows, :])
    each(4, lambda d: push(GAIN, gain_out, gains.at[x, z], along_z(d)))
    keep(GAIN, gain_out, gains.at[x, z])
    send_light(LK, 0, lk_ref, lk)

    def send_sq(d):
        to = yc(d)
        push(SQ, sq_ref.at[:, pl.ds(to * WIDE, WIDE)], sq.at[s], (to, h))

    each(8, send_sq)
    keep(SQ, sq_ref.at[:, pl.ds(s * WIDE, WIDE)], sq.at[s])

    landed(recv.at[KV], kv.at[pl.ds(0, 8 * PIECE)])

    def send_z(t, carry):
        block_rows = kv.at[pl.ds(t * SHARD + h * PIECE, PIECE)]
        each(4, lambda d: push(ZS, block_rows, block_rows, along_z(d), z_recv.at[t]))
        return carry

    lax.fori_loop(0, 3, send_z, 0)
    send_light(LV, 0, lv_ref, lv)
    lax.fori_loop(3, 5, send_z, 0)
    send_light(LK, 1, lk_ref, lk)
    lax.fori_loop(5, 7, send_z, 0)
    send_light(LV, 1, lv_ref, lv)
    lax.fori_loop(7, 8, send_z, 0)
    send_light(LQ, 0, lq_ref, lq)
    send_light(LQ, 1, lq_ref, lq)
    landed(recv.at[GAIN], gains.at[0])
    each(4, lambda d: push(GAINS, gains.at[x], gains.at[x], along_x(d)))

    def send_near(t):
        landed(z_recv.at[t], kv.at[pl.ds(0, 3 * PIECE)])
        block_rows = kv.at[pl.ds(t * SHARD + x * RUN, RUN)]
        push(XS, block_rows, block_rows, along_x(1), left_recv.at[t])
        push(XS, block_rows, block_rows, along_x(3), right_recv.at[t])

    def pass_on(t):
        landed(left_recv.at[t], kv.at[pl.ds(0, RUN)])
        landed(right_recv.at[t], kv.at[pl.ds(0, RUN)])
        way = 1 + 2 * (t % 2)
        block_rows = kv.at[pl.ds(t * SHARD + ((x + 4 - way) % 4) * RUN, RUN)]
        push(XS, block_rows, block_rows, along_x(way), far_recv.at[t])

    ends = []
    total = jnp.int32(0)
    for i in range(8):
        total = total + docs_ref[i] * 128
        ends.append(total)

    def doc_of(pos):
        found = jnp.zeros_like(pos)
        for end in ends:
            found = found + jnp.where(pos >= end, 1, 0)
        return found

    column = lax.broadcasted_iota(jnp.int32, (RUN, 1), 0)
    line = lax.broadcasted_iota(jnp.int32, (1, RUN), 1)
    causal = column >= line
    lower = jnp.where(causal, 1.0, 0.0).astype(BF16)

    def run_start(i):
        return (2 * y + i) * SHARD + x * RUN

    def sum_decays(i, carry):
        cum = jnp.dot(lower, dec[i], preferred_element_type=F32)
        cums[i] = cum
        tot[i] = jnp.broadcast_to(cum.T[0:8, RUN - 1:RUN], (8, 128))
        return carry

    def states(half):
        if half == 0:
            landed(recv.at[DEC], dec)
            lax.fori_loop(0, 2, sum_decays, 0)
        landed(recv.at[LK[half]], lk.at[0])
        landed(recv.at[LV[half]], lv.at[0])

        def add_states(i, carry):
            cum = cums[i]
            start = run_start(i)
            last = doc_of(start + RUN - 1)
            tail = jnp.exp(cum[RUN - 1:RUN, :] - cum)
            tail = tail * jnp.where(doc_of(start + column) == last, 1.0, 0.0)
            for j in range(4 * half, 4 * half + 4):
                cols = pl.ds(j * HD, HD)
                weighted = (lv[i, :, cols].astype(F32) * tail[:, j:j + 1]).astype(BF16)
                added = lax.dot_general(lk[i, :, cols], weighted, TN, preferred_element_type=F32)
                part[i, cols, :] = added.astype(BF16)
            return carry

        lax.fori_loop(0, 2, add_states, 0)

        def send_state(d):
            other, device = xy(d)
            if half == 0:
                push(TOT, tot, tots.at[y, :, x], device)
            mine = part.at[:, pl.ds(half * HALF + other * SLICE, SLICE), :]
            push(ST[half], mine, parts.at[half, y, :, x], device)

        each(16, send_state)
        if half == 0:
            keep(TOT, tot, tots.at[y, :, x])
        mine = part.at[:, pl.ds(half * HALF + member * SLICE, SLICE), :]
        keep(ST[half], mine, parts.at[half, y, :, x])

    def within(half):
        landed(recv.at[LQ[half]], lq.at[0])

        def inner_run(i, carry):
            cum = cums[i]
            across = cum.T
            start = run_start(i)
            allowed = causal & (doc_of(start + column) == doc_of(start + line))
            for j in range(4 * half, 4 * half + 4):
                cols = pl.ds(j * HD, HD)
                gap = cum[:, j:j + 1] - across[j:j + 1, :]
                weight = jnp.exp(jnp.where(allowed, gap, NEG))
                scores = lax.dot_general(
                    lq[i, :, cols], lk[i, :, cols], NT, preferred_element_type=F32
                )
                inner[i, :, cols] = jnp.dot(
                    (scores * weight).astype(BF16), lv[i, :, cols], preferred_element_type=F32
                )
            return carry

        lax.fori_loop(0, 2, inner_run, 0)

    def entering_states(half):
        if half == 0:
            landed(recv.at[TOT], tots)
        landed(recv.at[ST[half]], parts.at[half])

        def scan_runs(p, state):
            a, b, e = p // 8, (p // 4) % 2, p % 4
            back[half, a, b, e] = state.astype(BF16)
            start = p * RUN
            same = jnp.where(doc_of(start + RUN - 1) == doc_of(start - 1), 1.0, 0.0)
            factor = jnp.exp(tots[a, b, e, pl.ds(half * 4 + member // 4, 1), :]) * same
            return state * factor + parts[half, a, b, e].astype(F32)

        lax.fori_loop(0, 32, scan_runs, jnp.zeros((SLICE, HD), F32))
        place = incoming.at[:, pl.ds(half * HALF + member * SLICE, SLICE), :]

        def send_back(d):
            other, device = xy(d)
            push(IN[half], back.at[half, other // 4, :, other % 4], place, device)

        each(16, send_back)
        keep(IN[half], back.at[half, y, :, x], place)

    token = lax.broadcasted_iota(jnp.int32, (8 * PIECE, 1), 0) % PIECE
    key_line = lax.broadcasted_iota(jnp.int32, (1, SPAN), 1)

    def soft_piece(t):
        first = t * SHARD + h * PIECE
        doc_start = jnp.int32(0)
        for end in ends:
            doc_start = jnp.where(first >= end, end, doc_start)
        query = jnp.concatenate([sq[t, :, pl.ds(j * HD, HD)] for j in range(8)], axis=0)

        def block(k, stats, diagonal):
            top, denominator, acc = stats
            limit = first + PIECE - SPAN * k
            start = pl.multiple_of(jnp.maximum(limit - SPAN, 0), PIECE)
            key_pos = start + key_line
            scores = lax.dot_general(
                query, kv[pl.ds(start, SPAN), pl.ds(0, HD)], NT, preferred_element_type=F32
            )
            if diagonal:
                kept = (key_pos >= doc_start) & (key_pos <= first + token)
                scores = jnp.where(kept, scores, NEG)
            else:
                kept = (key_pos >= doc_start) & (key_pos < limit)
                scores = scores + jnp.where(kept, 0.0, NEG)
            new_top = jnp.maximum(top, jnp.max(scores, axis=1, keepdims=True))
            weights = jnp.exp2((scores - new_top) * SCALE)
            summed = jnp.sum(weights, axis=1, keepdims=True)
            product = jnp.dot(
                weights.astype(BF16), kv[pl.ds(start, SPAN), pl.ds(HD, HD)],
                preferred_element_type=F32,
            )
            rescale = jnp.exp2((top - new_top) * SCALE)
            return new_top, denominator * rescale + summed, acc * rescale + product

        stats = (
            jnp.full((8 * PIECE, 1), NEG, F32),
            jnp.zeros((8 * PIECE, 1), F32),
            jnp.zeros((8 * PIECE, HD), F32),
        )
        older = jnp.minimum(t, 3)
        stats = lax.fori_loop(0, older, lambda k, st: block(older - k, st, False), stats)
        landed(far_recv.at[t], kv.at[pl.ds(0, RUN)])
        top, denominator, acc = block(0, stats, True)
        result = (acc / denominator).astype(BF16)
        for j in range(8):
            sout[t, :, pl.ds(j * HD, HD)] = result[j * PIECE:(j + 1) * PIECE, :]

        target = so_ref.at[:, pl.ds(s * WIDE, WIDE)]

        @pl.when(t == s)
        def _():
            keep(SO, sout.at[t], target)

        @pl.when(t != s)
        def _():
            push(SO, sout.at[t], target, (t, h))

    def light_outputs(half):
        if half == 0:
            landed(recv.at[GAINS], gains.at[pl.ds(0, 3)])
        landed(recv.at[IN[half]], incoming.at[0])

        def finish(i, carry):
            start = run_start(i)
            carried = jnp.where(doc_of(start + column) == doc_of(start - 1), 1.0, 0.0)
            reach = jnp.exp(cums[i]) * carried
            for j in range(4 * half, 4 * half + 4):
                cols = pl.ds(j * HD, HD)
                entering = jnp.dot(
                    lq[i, :, cols], incoming[i, cols, :], preferred_element_type=F32
                )
                mixed = inner[i, :, cols] + entering * reach[:, j:j + 1]
                mean_square = jnp.mean(mixed * mixed, axis=1, keepdims=True)
                source = 2 * group + half
                gain = gains[source // 4, source % 4, pl.ds(j % 4, 1), :]
                lout[i, :, cols] = (mixed * lax.rsqrt(mean_square + 1e-6) * gain).astype(BF16)
            return carry

        lax.fori_loop(0, 2, finish, 0)
        cols = pl.ds(half * HALF, HALF)
        target = lo_ref.at[:, pl.ds(group * WIDE + half * HALF, HALF)]

        def send_out(d):
            other, device = zc(d)
            source = lout.at[other // 4, pl.ds((other % 4) * PIECE, PIECE), cols]
            push(LO[half], source, target, device)

        each(8, send_out)
        keep(LO[half], lout.at[c, rows, cols], target)

    def step(t, carry):
        def at(n, work, *args):
            pl.when(t == n)(lambda: work(*args))

        pl.when((t >= 2) & (t < 10))(lambda: pass_on(t - 2))
        at(2, states, 0)
        at(6, states, 1)
        pl.when(t < 8)(lambda: send_near(t))
        at(5, entering_states, 0)
        at(8, entering_states, 1)
        at(8, within, 0)
        at(8, light_outputs, 0)
        at(9, within, 1)
        at(10, light_outputs, 1)
        at(3, lambda: landed(recv.at[SQ], sq))
        pl.when(t >= 3)(lambda: soft_piece(t - 3))
        return carry

    lax.fori_loop(0, 11, step, 0)

    landed(send.at[KV], kv.at[pl.ds(0, 7 * PIECE)])
    landed(send.at[DEC], dec_out.at[pl.ds(0, 7)])
    landed(send.at[GAIN], gains.at[0, pl.ds(0, 3)])
    landed(send.at[GAINS], gains.at[pl.ds(0, 3)])
    for kind in LK + LV + LQ + LO:
        landed(send.at[kind], lk.at[0, pl.ds(0, 7 * 32), :])
    for kind in (SQ, SO):
        landed(send.at[kind], sq.at[pl.ds(0, 7)])
    landed(send.at[ZS], kv.at[pl.ds(0, 24 * PIECE)])
    landed(send.at[XS], kv.at[pl.ds(0, 24 * RUN)])
    landed(send.at[TOT], inner.at[0, pl.ds(0, 15 * 16), pl.ds(0, HD)])
    for kind in ST + IN:
        landed(send.at[kind], kv.at[pl.ds(0, 15 * SLICE)])
    for kind in LO:
        landed(recv.at[kind], lo_ref.at[:, pl.ds(0, 4 * WIDE)])
    landed(recv.at[SO], so_ref)


def per_device(
    light_query, light_key, light_value, light_decay, light_gain, soft_query, soft_kv, doc_blocks
):
    gain = light_gain.reshape(4, HD)
    kv = soft_kv.reshape(PIECE, 2 * WIDE)
    anywhere = pl.BlockSpec(memory_space=pl.ANY)
    vmem = pl.BlockSpec(memory_space=pltpu.VMEM)
    out = jax.ShapeDtypeStruct((PIECE, 8 * WIDE), BF16)
    scratch = [
        pltpu.VMEM((2, RUN, WIDE), BF16),
        pltpu.VMEM((2, RUN, WIDE), BF16),
        pltpu.VMEM((2, RUN, WIDE), BF16),
        pltpu.VMEM((8, PIECE, 128), BF16),
        pltpu.VMEM((2, RUN, 128), BF16),
        pltpu.VMEM((4, 4, 8, HD), F32),
        pltpu.VMEM((2, RUN, WIDE), F32),
        pltpu.VMEM((2, RUN, WIDE), BF16),
        pltpu.VMEM((2, WIDE, HD), BF16),
        pltpu.VMEM((2, 8, 128), F32),
        pltpu.VMEM((2, 4, 2, 4, SLICE, HD), BF16),
        pltpu.VMEM((4, 2, 4, 8, 128), F32),
        pltpu.VMEM((2, 4, 2, 4, SLICE, HD), BF16),
        pltpu.VMEM((2, WIDE, HD), BF16),
        pltpu.VMEM((8, PIECE, WIDE), BF16),
        pltpu.VMEM((8 * SHARD, 2 * HD), BF16),
        pltpu.VMEM((8, PIECE, WIDE), BF16),
        pltpu.VMEM((2, RUN, 128), F32),
        pltpu.VMEM((8, HD), F32),
        pltpu.SemaphoreType.DMA((KINDS,)),
        pltpu.SemaphoreType.DMA((KINDS,)),
        pltpu.SemaphoreType.DMA((8,)),
        pltpu.SemaphoreType.DMA((8,)),
        pltpu.SemaphoreType.DMA((8,)),
        pltpu.SemaphoreType.DMA((8,)),
    ]
    return pl.pallas_call(
        kernel,
        out_shape=(out, out),
        in_specs=[
            pl.BlockSpec(memory_space=pltpu.SMEM), anywhere, anywhere, anywhere, vmem, vmem,
            anywhere, anywhere,
        ],
        out_specs=(anywhere, anywhere),
        scratch_shapes=scratch,
        compiler_params=pltpu.CompilerParams(
            collective_id=0, has_side_effects=True, vmem_limit_bytes=63 * 2**20
        ),
    )(doc_blocks, light_query, light_key, light_value, light_decay, gain, soft_query, kv)


def solution(mesh):
    placed = (
        P(("seq", "head"), None),
        P(("seq", "head"), None),
        P(("seq", "head"), None),
        P(("seq", "head"), None),
        P("head"),
        P(("seq", "head"), None),
        P(("seq", "head"), None, None),
        P(),
    )
    return jax.shard_map(
        per_device,
        mesh=mesh,
        in_specs=placed,
        out_specs=(P(("seq", "head"), None), P(("seq", "head"), None)),
        check_vma=False,
    )
```

```python
import functools
import itertools
import math

import jax
import jax.numpy as jnp
from jax import lax
from jax.experimental import pallas as pl
from jax.experimental.pallas import tpu as pltpu
from jax.sharding import PartitionSpec as P

MESH = pl.DeviceIdType.MESH
F32, BF16 = jnp.float32, jnp.bfloat16
HD = 128
RUN = 256
PIECE = 64
WIDE = 1024
SHARD = 1024
SPAN = 1024
ROWS = 8 * PIECE
LOG2E = math.log2(math.e)
SCALE = LOG2E / math.sqrt(HD)
NEG = -1e30

KV, DEC, GAIN, GAINS, SQ, TOT, SO, ZS, XS = range(9)
LK, LV, LQ, ST, IN, LO = ((9 + 2 * i, 10 + 2 * i) for i in range(6))
KINDS = 21
SPLIT = ((0, 6), (6, 2))
SLICE = (48, 16)

NT = (((1,), (1,)), ((), ()))
TN = (((0,), (0,)), ((), ()))


def kernel(
    docs_ref, lq_ref, lk_ref, lv_ref, dec_ref, gain_ref, sq_ref, kv_ref,
    lo_ref, so_ref,
    lq, lk, lv, dec_out, dec, gains, inner, lout, part, tot, parts0, parts1, tots, back0, back1, incoming, factors,
    sq, kv, kv_out, sout, cums, gain_out, queries, marks, top, denominator, acc, send, recv, z_recv, left_recv, right_recv, far_recv,
):
    s = lax.axis_index("seq")
    h = lax.axis_index("head")
    y, c = s // 2, s % 2
    x, z = h // 4, h % 4
    group = c * 4 + z
    member = y * 4 + x

    parts, back = (parts0, parts1), (back0, back1)

    def part_cols(half, start=0):
        first, heads = SPLIT[half]
        return pl.ds(start + first * HD, heads * HD)

    def part_heads(half):
        first, heads = SPLIT[half]
        return range(first, first + heads)

    def yc(d):
        return (s + d) % 8

    def zc(d):
        other = (group + d) % 8
        return other, (y * 2 + other // 4, x * 4 + other % 4)

    def along_x(d):
        return (s, ((x + d) % 4) * 4 + z)

    def along_z(d):
        return (s, x * 4 + (z + d) % 4)

    def xy(d):
        other = (member + d) % 16
        return other, ((other // 4) * 2 + c, (other % 4) * 4 + z)

    def push(kind, src, dst, device, recv_sem=None):
        pltpu.make_async_remote_copy(
            src_ref=src, dst_ref=dst, send_sem=send.at[kind],
            recv_sem=recv.at[kind] if recv_sem is None else recv_sem,
            device_id=device, device_id_type=MESH,
        ).start()

    def keep(kind, src, dst):
        pltpu.make_async_copy(src, dst, recv.at[kind]).start()

    def landed(sem, ref):
        pltpu.make_async_copy(ref, ref, sem).wait()

    def each(n, body):
        def step(d, carry):
            body(d)
            return carry
        lax.fori_loop(1, n, step, 0)

    barrier = pltpu.get_barrier_semaphore()

    def greet(device):
        pl.semaphore_signal(barrier, inc=1, device_id=device, device_id_type=MESH)

    each(8, lambda d: greet((yc(d), h)))
    each(8, lambda d: greet(zc(d)[1]))
    each(16, lambda d: greet(xy(d)[1]))
    gain = gain_ref[...].astype(F32)
    gain_out[...] = jnp.concatenate([gain, gain], axis=0)
    wide = jnp.concatenate([dec_ref[...], dec_ref[...]], axis=1).astype(F32)
    for g in range(8):
        dec_out[g] = (wide if g == 0 else pltpu.roll(wide, 128 - 8 * g, 1)).astype(BF16)
    for g in range(8):
        for i in range(2):
            kv_out[g, :, pl.ds(i * HD, HD)] = kv_ref[:, i, pl.ds(g * HD, HD)]
    pl.semaphore_wait(barrier, 7 + 7 + 15)

    mine = pl.ds(SHARD + s * SHARD + h * PIECE, PIECE)

    def send_kv(d):
        to = yc(d)
        push(KV, kv_out.at[to], kv.at[mine], (to, h))

    each(8, send_kv)
    keep(KV, kv_out.at[s], kv.at[mine])

    rows = pl.ds(z * PIECE, PIECE)

    def send_light(kinds, half, ref, buf, some=None):
        first, heads = some or SPLIT[half]
        place = buf.at[c, rows, pl.ds(first * HD, heads * HD)]
        def one(d):
            other, device = zc(d)
            source = ref.at[:, pl.ds(other * WIDE + first * HD, heads * HD)]
            push(kinds[half], source, place, device)
        each(8, one)
        keep(kinds[half], ref.at[:, pl.ds(group * WIDE + first * HD, heads * HD)], place)

    def send_dec(d):
        other, device = zc(d)
        push(DEC, dec_out.at[other], dec.at[c, rows, :], device)

    each(8, send_dec)
    keep(DEC, dec_out.at[group], dec.at[c, rows, :])
    each(4, lambda d: push(GAIN, gain_out, gains.at[x, z], along_z(d)))
    keep(GAIN, gain_out, gains.at[x, z])
    send_light(LK, 0, lk_ref, lk, (0, 4))

    ends = []
    total = jnp.int32(0)
    for i in range(8):
        total = total + docs_ref[i] * 128
        ends.append(total)

    def doc_of(pos):
        found = jnp.zeros_like(pos)
        for end in ends:
            found = found + jnp.where(pos >= end, 1, 0)
        return found

    lane = lax.broadcasted_iota(jnp.int32, (1, HD), 1)
    doc_first = jnp.zeros((1, HD), jnp.int32)
    doc_end = jnp.zeros((1, HD), jnp.int32)
    for i, end in enumerate(ends):
        doc_first = jnp.where(lane == i, ends[i - 1] if i else 0, doc_first)
        doc_end = jnp.where(lane == i, end, doc_end)

    def mark(n, carry):
        at_row = pl.ds(pl.multiple_of(n * SHARD, SHARD), SHARD)
        row = lax.broadcasted_iota(jnp.int32, (SHARD, HD), 0)
        lanes = lax.broadcasted_iota(jnp.int32, (SHARD, HD), 1)
        token = (n - 1) * SHARD + row
        in_doc = (token >= doc_first) & (token < doc_end)
        own = (row == h * PIECE + lanes - 64) & (lanes >= 64)
        outside = (lanes == 8) & (token < 0)
        marks[at_row, :] = jnp.where(in_doc | own | outside, 1.0, 0.0).astype(BF16)
        return carry

    lax.fori_loop(0, 9, mark, 0)
    kv[pl.ds(0, SHARD), :] = jnp.zeros((SHARD, 2 * HD), BF16)

    landed(recv.at[KV], kv.at[pl.ds(0, 8 * PIECE)])

    def send_z(t, carry):
        block_rows = kv.at[pl.ds(SHARD + t * SHARD + h * PIECE, PIECE)]
        each(4, lambda d: push(ZS, block_rows, block_rows, along_z(d), z_recv.at[t]))
        return carry

    lax.fori_loop(0, 4, send_z, 0)
    def send_sq(d):
        to = yc(d)
        push(SQ, sq_ref.at[:, pl.ds(to * WIDE, WIDE)], sq.at[s], (to, h))

    each(8, send_sq)
    keep(SQ, sq_ref.at[:, pl.ds(s * WIDE, WIDE)], sq.at[s])

    send_light(LK, 0, lk_ref, lk, (4, 2))
    send_light(LV, 0, lv_ref, lv)
    lax.fori_loop(4, 6, send_z, 0)
    send_light(LK, 1, lk_ref, lk)
    send_light(LV, 1, lv_ref, lv)
    lax.fori_loop(6, 8, send_z, 0)
    send_light(LQ, 0, lq_ref, lq)
    send_light(LQ, 1, lq_ref, lq)
    landed(recv.at[GAIN], gains.at[0])
    each(4, lambda d: push(GAINS, gains.at[x], gains.at[x], along_x(d)))

    def continues(p, carry):
        same = jnp.where(doc_of(p * RUN + RUN - 1) == doc_of(p * RUN - 1), 1.0, 0.0)
        factors[p // 8, (p // 4) % 2, p % 4] = jnp.full((8, 128), same, F32)
        return carry

    def prepare():
        lax.fori_loop(0, 32, continues, 0)
        top[...] = jnp.full_like(top, NEG)
        denominator[...] = jnp.zeros_like(denominator)
        acc[...] = jnp.zeros_like(acc)

    def send_near(t):
        landed(z_recv.at[t], kv.at[pl.ds(0, 3 * PIECE)])
        block_rows = kv.at[pl.ds(SHARD + t * SHARD + x * RUN, RUN)]
        push(XS, block_rows, block_rows, along_x(1), left_recv.at[t])
        push(XS, block_rows, block_rows, along_x(3), right_recv.at[t])

    def pass_on(t):
        landed(left_recv.at[t], kv.at[pl.ds(0, RUN)])
        landed(right_recv.at[t], kv.at[pl.ds(0, RUN)])
        way = 1 + 2 * (t % 2)
        block_rows = kv.at[pl.ds(SHARD + t * SHARD + ((x + 4 - way) % 4) * RUN, RUN)]
        push(XS, block_rows, block_rows, along_x(way), far_recv.at[t])

    column = lax.broadcasted_iota(jnp.int32, (RUN, 1), 0)
    line = lax.broadcasted_iota(jnp.int32, (1, RUN), 1)
    causal = column >= line
    lower = jnp.where(causal, 1.0, 0.0).astype(BF16)

    def run_start(i):
        return (2 * y + i) * SHARD + x * RUN

    def sum_decays(i, carry):
        cum = jnp.dot(lower, dec[i], preferred_element_type=F32)
        cums[i] = cum
        tot[i] = jnp.broadcast_to(cum.T[0:8, RUN - 1:RUN], (8, 128))
        return carry

    def slice_rows(half, owner):
        return pl.ds(SPLIT[half][0] * HD + owner * SLICE[half], SLICE[half])

    def states(half):
        if half == 0:
            landed(recv.at[DEC], dec)
            lax.fori_loop(0, 2, sum_decays, 0)
        landed(recv.at[LK[half]], lk.at[:, :, part_cols(half)])
        landed(recv.at[LV[half]], lv.at[:, :, part_cols(half)])

        def add_states(i, carry):
            cum = cums[i]
            start = run_start(i)
            last = doc_of(start + RUN - 1)
            tail = jnp.exp(cum[RUN - 1:RUN, :] - cum)
            tail = tail * jnp.where(doc_of(start + column) == last, 1.0, 0.0)
            for j in part_heads(half):
                cols = pl.ds(j * HD, HD)
                weighted = (lv[i, :, cols].astype(F32) * tail[:, j:j + 1]).astype(BF16)
                added = lax.dot_general(lk[i, :, cols], weighted, TN, preferred_element_type=F32)
                part[i, cols, :] = added.astype(BF16)
            return carry

        lax.fori_loop(0, 2, add_states, 0)

        def send_state(d):
            other, device = xy(d)
            if half == 0:
                push(TOT, tot, tots.at[y, :, x], device)
            mine = part.at[:, slice_rows(half, other), :]
            push(ST[half], mine, parts[half].at[y, :, x], device)

        each(16, send_state)
        if half == 0:
            keep(TOT, tot, tots.at[y, :, x])
        mine = part.at[:, slice_rows(half, member), :]
        keep(ST[half], mine, parts[half].at[y, :, x])

    def within(half):
        landed(recv.at[LQ[half]], lq.at[:, :, part_cols(half)])

        def inner_run(i, carry):
            cum = cums[i]
            across = cum.T
            start = run_start(i)
            allowed = causal & (doc_of(start + column) == doc_of(start + line))
            for j in part_heads(half):
                cols = pl.ds(j * HD, HD)
                gap = cum[:, j:j + 1] - across[j:j + 1, :]
                weight = jnp.exp(jnp.where(allowed, gap, NEG))
                scores = lax.dot_general(
                    lq[i, :, cols], lk[i, :, cols], NT, preferred_element_type=F32
                )
                inner[i, :, cols] = jnp.dot(
                    (scores * weight).astype(BF16), lv[i, :, cols], preferred_element_type=F32
                )
            return carry

        lax.fori_loop(0, 2, inner_run, 0)

    def entering_states(half):
        if half == 0:
            landed(recv.at[TOT], tots)
            factors[...] = factors[...] * jnp.exp(tots[...])
        landed(recv.at[ST[half]], parts[half])
        own_first = member * SLICE[half]
        head = own_first // HD
        after = jnp.minimum(head + 1, SPLIT[half][1] - 1)
        in_head = own_first + lax.broadcasted_iota(jnp.int32, (SLICE[half], HD), 0) < (head + 1) * HD

        state = jnp.zeros((SLICE[half], HD), F32)
        for a, b, e in itertools.product(range(4), range(2), range(4)):
            back[half][a, b, e] = state.astype(BF16)
            one = factors[a, b, e, pl.ds(SPLIT[half][0] + head, 1), :]
            two = factors[a, b, e, pl.ds(SPLIT[half][0] + after, 1), :]
            state = state * jnp.where(in_head, one, two) + parts[half][a, b, e].astype(F32)
        place = incoming.at[:, slice_rows(half, member), :]

        def send_back(d):
            other, device = xy(d)
            push(IN[half], back[half].at[other // 4, :, other % 4], place, device)

        each(16, send_back)
        keep(IN[half], back[half].at[y, :, x], place)

    def take_queries(t, carry):
        first = t * SHARD + h * PIECE
        inside = (first >= doc_first) & (first < doc_end)
        kept = jnp.where((lane > 8) | inside, 0.0, NEG).astype(BF16)
        for j in range(8):
            at_row = pl.ds(pl.multiple_of(t * ROWS, ROWS) + j * PIECE, PIECE)
            queries[at_row, pl.ds(0, HD)] = sq[t, :, pl.ds(j * HD, HD)]
            queries[at_row, pl.ds(HD, HD)] = jnp.broadcast_to(kept, (PIECE, HD))
        return carry

    def all_queries():
        landed(recv.at[SQ], sq)
        lax.fori_loop(0, 8, take_queries, 0)

    def key_block(t, count):
        first_row = pl.multiple_of(t * ROWS, ROWS)
        at_rows = pl.ds(first_row, count * ROWS)
        start = pl.multiple_of(t * SHARD + h * PIECE + PIECE, PIECE)
        keys = jnp.concatenate(
            [kv[pl.ds(start, SPAN), pl.ds(0, HD)], marks[pl.ds(start, SPAN), :]], axis=1
        )
        scores = lax.dot_general(queries[at_rows, :], keys, NT, preferred_element_type=F32)
        tiles = [scores[:, i * HD:(i + 1) * HD] for i in range(SPAN // HD)]
        highest = functools.reduce(jnp.maximum, tiles)
        old = top[at_rows, :]
        new = jnp.maximum(old, jnp.broadcast_to(jnp.max(highest, axis=1, keepdims=True), old.shape))
        top[at_rows, :] = new
        rescale = jnp.exp2((old - new) * SCALE)
        weights = [jnp.exp2((tile - new) * SCALE) for tile in tiles]
        denominator[at_rows, :] = functools.reduce(jnp.add, weights, denominator[at_rows, :] * rescale)
        rounded = jnp.concatenate([w.astype(BF16) for w in weights], axis=1)
        product = jnp.dot(rounded, kv[pl.ds(start, SPAN), pl.ds(HD, HD)], preferred_element_type=F32)
        acc[at_rows, :] = acc[at_rows, :] * rescale + product

    def soft_piece(t):
        landed(far_recv.at[t], kv.at[pl.ds(0, RUN)])
        at_rows = pl.ds(pl.multiple_of(t * ROWS, ROWS), ROWS)
        token = lax.broadcasted_iota(jnp.int32, (ROWS, HD), 0) % PIECE
        lanes = lax.broadcasted_iota(jnp.int32, (ROWS, HD), 1)
        kept = queries[at_rows, pl.ds(HD, HD)].astype(F32)
        queries[at_rows, pl.ds(HD, HD)] = jnp.where(lanes - 64 > token, NEG, kept).astype(BF16)
        pl.when(t <= 4)(lambda: key_block(t, 4))
        for last in (5, 6, 7):
            pl.when(t == last)(functools.partial(key_block, t, 8 - last))
        whole = jnp.sum(denominator[at_rows, :], axis=1, keepdims=True)
        result = (acc[at_rows, :] / whole).astype(BF16)
        for j in range(8):
            sout[t, :, pl.ds(j * HD, HD)] = result[j * PIECE:(j + 1) * PIECE, :]

        target = so_ref.at[:, pl.ds(s * WIDE, WIDE)]

        @pl.when(t == s)
        def _():
            keep(SO, sout.at[t], target)

        @pl.when(t != s)
        def _():
            push(SO, sout.at[t], target, (t, h))

    def light_outputs(half):
        if half == 0:
            landed(recv.at[GAINS], gains.at[pl.ds(0, 3)])
        landed(recv.at[IN[half]], incoming.at[:, part_cols(half), :])

        def finish(i, carry):
            start = run_start(i)
            carried = jnp.where(doc_of(start + column) == doc_of(start - 1), 1.0, 0.0)
            reach = jnp.exp(cums[i]) * carried
            for j in part_heads(half):
                cols = pl.ds(j * HD, HD)
                entering = jnp.dot(
                    lq[i, :, cols], incoming[i, cols, :], preferred_element_type=F32
                )
                mixed = inner[i, :, cols] + entering * reach[:, j:j + 1]
                mean_square = jnp.mean(mixed * mixed, axis=1, keepdims=True)
                source = 2 * group + j // 4
                gain = gains[source // 4, source % 4, pl.ds(j % 4, 1), :]
                lout[i, :, cols] = (mixed * lax.rsqrt(mean_square + 1e-6) * gain).astype(BF16)
            return carry

        lax.fori_loop(0, 2, finish, 0)
        cols = part_cols(half)
        target = lo_ref.at[:, part_cols(half, group * WIDE)]

        def send_out(d):
            other, device = zc(d)
            source = lout.at[other // 4, pl.ds((other % 4) * PIECE, PIECE), cols]
            push(LO[half], source, target, device)

        each(8, send_out)
        keep(LO[half], lout.at[c, rows, cols], target)

    def step(t, carry):
        def at(n, work, *args):
            pl.when(t == n)(lambda: work(*args))

        pl.when(t < 4)(lambda: send_near(t))
        pl.when((t >= 2) & (t < 5))(lambda: pass_on(t - 2))
        at(3, prepare)
        at(3, all_queries)
        pl.when(t >= 4)(lambda: soft_piece(t - 4))
        at(4, states, 0)
        at(4, send_near, 4)
        at(4, send_near, 5)
        at(4, pass_on, 3)
        at(6, states, 1)
        at(6, send_near, 6)
        at(7, entering_states, 0)
        at(7, send_near, 7)
        pl.when((t >= 6) & (t < 10))(lambda: pass_on(t - 2))
        at(8, entering_states, 1)
        at(8, within, 0)
        at(8, light_outputs, 0)
        at(9, within, 1)
        at(9, light_outputs, 1)
        return carry

    lax.fori_loop(0, 12, step, 0)

    landed(send.at[KV], kv.at[pl.ds(0, 7 * PIECE)])
    landed(send.at[DEC], dec_out.at[pl.ds(0, 7)])
    landed(send.at[GAIN], gains.at[0, pl.ds(0, 3)])
    landed(send.at[GAINS], gains.at[pl.ds(0, 3)])
    for kinds in (LK, LV, LQ, LO):
        for half in range(2):
            landed(send.at[kinds[half]], lk.at[:, pl.ds(0, 7 * 32), part_cols(half)])
    for kind in (SQ, SO):
        landed(send.at[kind], sq.at[pl.ds(0, 7)])
    landed(send.at[ZS], kv.at[pl.ds(0, 24 * PIECE)])
    landed(send.at[XS], kv.at[pl.ds(0, 24 * RUN)])
    landed(send.at[TOT], inner.at[0, pl.ds(0, 15 * 16), pl.ds(0, HD)])
    for half in range(2):
        for kind in (ST[half], IN[half]):
            landed(send.at[kind], kv.at[pl.ds(0, 15 * SLICE[half])])
        landed(recv.at[LO[half]], lo_ref.at[:, pl.ds(0, 8 * SPLIT[half][1] * HD)])
    landed(recv.at[SO], so_ref)


def per_device(
    light_query, light_key, light_value, light_decay, light_gain, soft_query, soft_kv, doc_blocks
):
    gain = light_gain.reshape(4, HD)
    anywhere = pl.BlockSpec(memory_space=pl.ANY)
    vmem = pl.BlockSpec(memory_space=pltpu.VMEM)
    out = jax.ShapeDtypeStruct((PIECE, 8 * WIDE), BF16)
    scratch = [
        pltpu.VMEM((2, RUN, WIDE), BF16),
        pltpu.VMEM((2, RUN, WIDE), BF16),
        pltpu.VMEM((2, RUN, WIDE), BF16),
        pltpu.VMEM((8, PIECE, 128), BF16),
        pltpu.VMEM((2, RUN, 128), BF16),
        pltpu.VMEM((4, 4, 8, HD), F32),
        pltpu.VMEM((2, RUN, WIDE), F32),
        pltpu.VMEM((2, RUN, WIDE), BF16),
        pltpu.VMEM((2, WIDE, HD), BF16),
        pltpu.VMEM((2, 8, 128), F32),
        pltpu.VMEM((4, 2, 4, SLICE[0], HD), BF16),
        pltpu.VMEM((4, 2, 4, SLICE[1], HD), BF16),
        pltpu.VMEM((4, 2, 4, 8, 128), F32),
        pltpu.VMEM((4, 2, 4, SLICE[0], HD), BF16),
        pltpu.VMEM((4, 2, 4, SLICE[1], HD), BF16),
        pltpu.VMEM((2, WIDE, HD), BF16),
        pltpu.VMEM((4, 2, 4, 8, 128), F32),
        pltpu.VMEM((8, PIECE, WIDE), BF16),
        pltpu.VMEM((9 * SHARD, 2 * HD), BF16),
        pltpu.VMEM((8, PIECE, 2 * HD), BF16),
        pltpu.VMEM((8, PIECE, WIDE), BF16),
        pltpu.VMEM((2, RUN, 128), F32),
        pltpu.VMEM((8, HD), F32),
        pltpu.VMEM((8 * ROWS, 2 * HD), BF16),
        pltpu.VMEM((9 * SHARD, HD), BF16),
        pltpu.VMEM((8 * ROWS, HD), F32),
        pltpu.VMEM((8 * ROWS, HD), F32),
        pltpu.VMEM((8 * ROWS, HD), F32),
        pltpu.SemaphoreType.DMA((KINDS,)),
        pltpu.SemaphoreType.DMA((KINDS,)),
        pltpu.SemaphoreType.DMA((8,)),
        pltpu.SemaphoreType.DMA((8,)),
        pltpu.SemaphoreType.DMA((8,)),
        pltpu.SemaphoreType.DMA((8,)),
    ]
    return pl.pallas_call(
        kernel,
        out_shape=(out, out),
        in_specs=[
            pl.BlockSpec(memory_space=pltpu.SMEM), anywhere, anywhere, anywhere, vmem, vmem,
            anywhere, vmem,
        ],
        out_specs=(anywhere, anywhere),
        scratch_shapes=scratch,
        compiler_params=pltpu.CompilerParams(
            collective_id=0, has_side_effects=True, vmem_limit_bytes=63 * 2**20
        ),
    )(doc_blocks, light_query, light_key, light_value, light_decay, gain, soft_query, soft_kv)


def solution(mesh):
    placed = (
        P(("seq", "head"), None),
        P(("seq", "head"), None),
        P(("seq", "head"), None),
        P(("seq", "head"), None),
        P("head"),
        P(("seq", "head"), None),
        P(("seq", "head"), None, None),
        P(),
    )
    return jax.shard_map(
        per_device,
        mesh=mesh,
        in_specs=placed,
        out_specs=(P(("seq", "head"), None), P(("seq", "head"), None)),
        check_vma=False,
    )
```

```python
import functools
import itertools
import math

import jax
import jax.numpy as jnp
from jax import lax
from jax.experimental import pallas as pl
from jax.experimental.pallas import tpu as pltpu
from jax.sharding import PartitionSpec as P

MESH = pl.DeviceIdType.MESH
F32, BF16 = jnp.float32, jnp.bfloat16
HD = 128
RUN = 256
PIECE = 64
WIDE = 1024
SHARD = 1024
SPAN = 1024
ROWS = 8 * PIECE
LOG2E = math.log2(math.e)
SCALE = LOG2E / math.sqrt(HD)
NEG = -1e30

KV, DEC, GAIN, GAINS, SQ, TOT, SO, ZS, XS = range(9)
LK, LV, LQ, ST, IN, LO = ((9 + 2 * i, 10 + 2 * i) for i in range(6))
KINDS = 21
SPLIT = ((0, 6), (6, 2))
SLICE = (48, 16)

NT = (((1,), (1,)), ((), ()))
TN = (((0,), (0,)), ((), ()))


def kernel(
    docs_ref, lq_ref, lk_ref, lv_ref, dec_ref, gain_ref, sq_ref, kv_ref,
    lo_ref, so_ref,
    lq, lk, lv, dec_out, dec, gains, inner, lout, part, tot, parts0, parts1, tots, back0, back1, incoming, factors,
    sq, kv, kv_out, sout, cums, gain_out, queries, marks, top, denominator, acc, send, recv, kv_recv, z_recv, left_recv, right_recv, far_recv,
):
    s = lax.axis_index("seq")
    h = lax.axis_index("head")
    y, c = s // 2, s % 2
    x, z = h // 4, h % 4
    group = c * 4 + z
    member = y * 4 + x

    parts, back = (parts0, parts1), (back0, back1)

    def part_cols(half, start=0):
        first, heads = SPLIT[half]
        return pl.ds(start + first * HD, heads * HD)

    def part_heads(half):
        first, heads = SPLIT[half]
        return range(first, first + heads)

    def yc(d):
        return (s + d) % 8

    def zc(d):
        other = (group + d) % 8
        return other, (y * 2 + other // 4, x * 4 + other % 4)

    def along_x(d):
        return (s, ((x + d) % 4) * 4 + z)

    def along_z(d):
        return (s, x * 4 + (z + d) % 4)

    def xy(d):
        other = (member + d) % 16
        return other, ((other // 4) * 2 + c, (other % 4) * 4 + z)

    def push(kind, src, dst, device, recv_sem=None):
        pltpu.make_async_remote_copy(
            src_ref=src, dst_ref=dst, send_sem=send.at[kind],
            recv_sem=recv.at[kind] if recv_sem is None else recv_sem,
            device_id=device, device_id_type=MESH,
        ).start()

    def keep(kind, src, dst):
        pltpu.make_async_copy(src, dst, recv.at[kind]).start()

    def landed(sem, ref):
        pltpu.make_async_copy(ref, ref, sem).wait()

    def each(n, body):
        def step(d, carry):
            body(d)
            return carry
        lax.fori_loop(1, n, step, 0)

    barrier = pltpu.get_barrier_semaphore()

    def greet(device):
        pl.semaphore_signal(barrier, inc=1, device_id=device, device_id_type=MESH)

    each(8, lambda d: greet((yc(d), h)))
    each(8, lambda d: greet(zc(d)[1]))
    each(16, lambda d: greet(xy(d)[1]))
    gain = gain_ref[...].astype(F32)
    gain_out[...] = jnp.concatenate([gain, gain], axis=0)
    wide = jnp.concatenate([dec_ref[...], dec_ref[...]], axis=1).astype(F32)
    for g in range(8):
        dec_out[g] = (wide if g == 0 else pltpu.roll(wide, 128 - 8 * g, 1)).astype(BF16)
    for g in range(8):
        for i in range(2):
            kv_out[g, :, pl.ds(i * HD, HD)] = kv_ref[:, i, pl.ds(g * HD, HD)]
    pl.semaphore_wait(barrier, 7 + 7 + 15)

    mine = pl.ds(SHARD + s * SHARD + h * PIECE, PIECE)

    def send_kv(d):
        to = yc(d)
        push(KV, kv_out.at[to], kv.at[mine], (to, h), kv_recv.at[s])

    each(8, send_kv)
    pltpu.make_async_copy(kv_out.at[s], kv.at[mine], kv_recv.at[s]).start()

    rows = pl.ds(z * PIECE, PIECE)

    def send_light(kinds, half, ref, buf, some=None):
        first, heads = some or SPLIT[half]
        place = buf.at[c, rows, pl.ds(first * HD, heads * HD)]
        def one(d):
            other, device = zc(d)
            source = ref.at[:, pl.ds(other * WIDE + first * HD, heads * HD)]
            push(kinds[half], source, place, device)
        each(8, one)
        keep(kinds[half], ref.at[:, pl.ds(group * WIDE + first * HD, heads * HD)], place)

    def send_dec(d):
        other, device = zc(d)
        push(DEC, dec_out.at[other], dec.at[c, rows, :], device)

    send_light(LK, 0, lk_ref, lk, (0, 2))

    ends = []
    total = jnp.int32(0)
    for i in range(8):
        total = total + docs_ref[i] * 128
        ends.append(total)

    def doc_of(pos):
        found = jnp.zeros_like(pos)
        for end in ends:
            found = found + jnp.where(pos >= end, 1, 0)
        return found

    lane = lax.broadcasted_iota(jnp.int32, (1, HD), 1)
    doc_first = jnp.zeros((1, HD), jnp.int32)
    doc_end = jnp.zeros((1, HD), jnp.int32)
    for i, end in enumerate(ends):
        doc_first = jnp.where(lane == i, ends[i - 1] if i else 0, doc_first)
        doc_end = jnp.where(lane == i, end, doc_end)

    def mark(n, carry):
        at_row = pl.ds(pl.multiple_of(n * SHARD, SHARD), SHARD)
        row = lax.broadcasted_iota(jnp.int32, (SHARD, HD), 0)
        lanes = lax.broadcasted_iota(jnp.int32, (SHARD, HD), 1)
        token = (n - 1) * SHARD + row
        in_doc = (token >= doc_first) & (token < doc_end)
        own = (row == h * PIECE + lanes - 64) & (lanes >= 64)
        outside = (lanes == 8) & (token < 0)
        marks[at_row, :] = jnp.where(in_doc | own | outside, 1.0, 0.0).astype(BF16)
        return carry

    lax.fori_loop(0, 9, mark, 0)
    kv[pl.ds(0, SHARD), :] = jnp.zeros((SHARD, 2 * HD), BF16)


    def send_z(t, carry):
        landed(kv_recv.at[t], kv.at[pl.ds(0, PIECE)])
        block_rows = kv.at[pl.ds(SHARD + t * SHARD + h * PIECE, PIECE)]
        each(4, lambda d: push(ZS, block_rows, block_rows, along_z(d), z_recv.at[t]))
        return carry

    lax.fori_loop(0, 4, send_z, 0)
    def send_sq(d):
        to = yc(d)
        push(SQ, sq_ref.at[:, pl.ds(to * WIDE, WIDE)], sq.at[s], (to, h))

    each(8, send_sq)
    keep(SQ, sq_ref.at[:, pl.ds(s * WIDE, WIDE)], sq.at[s])

    each(8, send_dec)
    keep(DEC, dec_out.at[group], dec.at[c, rows, :])
    each(4, lambda d: push(GAIN, gain_out, gains.at[x, z], along_z(d)))
    keep(GAIN, gain_out, gains.at[x, z])
    send_light(LK, 0, lk_ref, lk, (2, 4))
    send_light(LV, 0, lv_ref, lv)
    def pass_gains():
        landed(recv.at[GAIN], gains.at[0])
        each(4, lambda d: push(GAINS, gains.at[x], gains.at[x], along_x(d)))


    def continues(p, carry):
        same = jnp.where(doc_of(p * RUN + RUN - 1) == doc_of(p * RUN - 1), 1.0, 0.0)
        factors[p // 8, (p // 4) % 2, p % 4] = jnp.full((8, 128), same, F32)
        return carry

    def prepare():
        lax.fori_loop(0, 32, continues, 0)
        top[...] = jnp.full_like(top, NEG)
        denominator[...] = jnp.zeros_like(denominator)
        acc[...] = jnp.zeros_like(acc)

    def send_near(t):
        landed(z_recv.at[t], kv.at[pl.ds(0, 3 * PIECE)])
        block_rows = kv.at[pl.ds(SHARD + t * SHARD + x * RUN, RUN)]
        push(XS, block_rows, block_rows, along_x(1), left_recv.at[t])
        push(XS, block_rows, block_rows, along_x(3), right_recv.at[t])

    def pass_on(t):
        landed(left_recv.at[t], kv.at[pl.ds(0, RUN)])
        landed(right_recv.at[t], kv.at[pl.ds(0, RUN)])
        way = 1 + 2 * (t % 2)
        block_rows = kv.at[pl.ds(SHARD + t * SHARD + ((x + 4 - way) % 4) * RUN, RUN)]
        push(XS, block_rows, block_rows, along_x(way), far_recv.at[t])

    column = lax.broadcasted_iota(jnp.int32, (RUN, 1), 0)
    line = lax.broadcasted_iota(jnp.int32, (1, RUN), 1)
    causal = column >= line
    lower = jnp.where(causal, 1.0, 0.0).astype(BF16)

    def run_start(i):
        return (2 * y + i) * SHARD + x * RUN

    def sum_decays(i, carry):
        cum = jnp.dot(lower, dec[i], preferred_element_type=F32)
        cums[i] = cum
        tot[i] = jnp.broadcast_to(cum.T[0:8, RUN - 1:RUN], (8, 128))
        return carry

    def slice_rows(half, owner):
        return pl.ds(SPLIT[half][0] * HD + owner * SLICE[half], SLICE[half])

    def states(half):
        if half == 0:
            landed(recv.at[DEC], dec)
            lax.fori_loop(0, 2, sum_decays, 0)
        landed(recv.at[LK[half]], lk.at[:, :, part_cols(half)])
        landed(recv.at[LV[half]], lv.at[:, :, part_cols(half)])

        def add_states(i, carry):
            cum = cums[i]
            start = run_start(i)
            last = doc_of(start + RUN - 1)
            tail = jnp.exp(cum[RUN - 1:RUN, :] - cum)
            tail = tail * jnp.where(doc_of(start + column) == last, 1.0, 0.0)
            for j in part_heads(half):
                cols = pl.ds(j * HD, HD)
                weighted = (lv[i, :, cols].astype(F32) * tail[:, j:j + 1]).astype(BF16)
                added = lax.dot_general(lk[i, :, cols], weighted, TN, preferred_element_type=F32)
                part[i, cols, :] = added.astype(BF16)
            return carry

        lax.fori_loop(0, 2, add_states, 0)

        def send_state(d):
            other, device = xy(d)
            if half == 0:
                push(TOT, tot, tots.at[y, :, x], device)
            mine = part.at[:, slice_rows(half, other), :]
            push(ST[half], mine, parts[half].at[y, :, x], device)

        each(16, send_state)
        if half == 0:
            keep(TOT, tot, tots.at[y, :, x])
        mine = part.at[:, slice_rows(half, member), :]
        keep(ST[half], mine, parts[half].at[y, :, x])

    def within(half):
        landed(recv.at[LQ[half]], lq.at[:, :, part_cols(half)])

        def inner_run(i, carry):
            cum = cums[i]
            across = cum.T
            start = run_start(i)
            allowed = causal & (doc_of(start + column) == doc_of(start + line))
            for j in part_heads(half):
                cols = pl.ds(j * HD, HD)
                gap = cum[:, j:j + 1] - across[j:j + 1, :]
                weight = jnp.exp(jnp.where(allowed, gap, NEG))
                scores = lax.dot_general(
                    lq[i, :, cols], lk[i, :, cols], NT, preferred_element_type=F32
                )
                inner[i, :, cols] = jnp.dot(
                    (scores * weight).astype(BF16), lv[i, :, cols], preferred_element_type=F32
                )
            return carry

        lax.fori_loop(0, 2, inner_run, 0)

    def entering_states(half):
        if half == 0:
            landed(recv.at[TOT], tots)
            factors[...] = factors[...] * jnp.exp(tots[...])
        landed(recv.at[ST[half]], parts[half])
        own_first = member * SLICE[half]
        head = own_first // HD
        after = jnp.minimum(head + 1, SPLIT[half][1] - 1)
        in_head = own_first + lax.broadcasted_iota(jnp.int32, (SLICE[half], HD), 0) < (head + 1) * HD

        state = jnp.zeros((SLICE[half], HD), F32)
        for a, b, e in itertools.product(range(4), range(2), range(4)):
            back[half][a, b, e] = state.astype(BF16)
            one = factors[a, b, e, pl.ds(SPLIT[half][0] + head, 1), :]
            two = factors[a, b, e, pl.ds(SPLIT[half][0] + after, 1), :]
            state = state * jnp.where(in_head, one, two) + parts[half][a, b, e].astype(F32)
        place = incoming.at[:, slice_rows(half, member), :]

        def send_back(d):
            other, device = xy(d)
            push(IN[half], back[half].at[other // 4, :, other % 4], place, device)

        each(16, send_back)
        keep(IN[half], back[half].at[y, :, x], place)

    def take_queries(t, carry):
        first = t * SHARD + h * PIECE
        inside = (first >= doc_first) & (first < doc_end)
        kept = jnp.where((lane > 8) | inside, 0.0, NEG).astype(BF16)
        for j in range(8):
            at_row = pl.ds(pl.multiple_of(t * ROWS, ROWS) + j * PIECE, PIECE)
            queries[at_row, pl.ds(0, HD)] = sq[t, :, pl.ds(j * HD, HD)]
            queries[at_row, pl.ds(HD, HD)] = jnp.broadcast_to(kept, (PIECE, HD))
        return carry

    def all_queries():
        landed(recv.at[SQ], sq)
        lax.fori_loop(0, 8, take_queries, 0)

    def key_block(t, count):
        first_row = pl.multiple_of(t * ROWS, ROWS)
        at_rows = pl.ds(first_row, count * ROWS)
        start = pl.multiple_of(t * SHARD + h * PIECE + PIECE, PIECE)
        keys = jnp.concatenate(
            [kv[pl.ds(start, SPAN), pl.ds(0, HD)], marks[pl.ds(start, SPAN), :]], axis=1
        )
        scores = lax.dot_general(queries[at_rows, :], keys, NT, preferred_element_type=F32)
        tiles = [scores[:, i * HD:(i + 1) * HD] for i in range(SPAN // HD)]
        highest = functools.reduce(jnp.maximum, tiles)
        old = top[at_rows, :]
        new = jnp.maximum(old, jnp.broadcast_to(jnp.max(highest, axis=1, keepdims=True), old.shape))
        top[at_rows, :] = new
        rescale = jnp.exp2((old - new) * SCALE)
        weights = [jnp.exp2((tile - new) * SCALE) for tile in tiles]
        denominator[at_rows, :] = functools.reduce(jnp.add, weights, denominator[at_rows, :] * rescale)
        rounded = jnp.concatenate([w.astype(BF16) for w in weights], axis=1)
        product = jnp.dot(rounded, kv[pl.ds(start, SPAN), pl.ds(HD, HD)], preferred_element_type=F32)
        acc[at_rows, :] = acc[at_rows, :] * rescale + product

    def soft_piece(t):
        landed(far_recv.at[t], kv.at[pl.ds(0, RUN)])
        at_rows = pl.ds(pl.multiple_of(t * ROWS, ROWS), ROWS)
        token = lax.broadcasted_iota(jnp.int32, (ROWS, HD), 0) % PIECE
        lanes = lax.broadcasted_iota(jnp.int32, (ROWS, HD), 1)
        kept = queries[at_rows, pl.ds(HD, HD)].astype(F32)
        queries[at_rows, pl.ds(HD, HD)] = jnp.where(lanes - 64 > token, NEG, kept).astype(BF16)
        pl.when(t <= 4)(lambda: key_block(t, 4))
        for last in (5, 6, 7):
            pl.when(t == last)(functools.partial(key_block, t, 8 - last))
        whole = jnp.sum(denominator[at_rows, :], axis=1, keepdims=True)
        result = (acc[at_rows, :] / whole).astype(BF16)
        for j in range(8):
            sout[t, :, pl.ds(j * HD, HD)] = result[j * PIECE:(j + 1) * PIECE, :]

        target = so_ref.at[:, pl.ds(s * WIDE, WIDE)]

        @pl.when(t == s)
        def _():
            keep(SO, sout.at[t], target)

        @pl.when(t != s)
        def _():
            push(SO, sout.at[t], target, (t, h))

    def light_outputs(half):
        if half == 0:
            landed(recv.at[GAINS], gains.at[pl.ds(0, 3)])
        landed(recv.at[IN[half]], incoming.at[:, part_cols(half), :])

        def finish(i, carry):
            start = run_start(i)
            carried = jnp.where(doc_of(start + column) == doc_of(start - 1), 1.0, 0.0)
            reach = jnp.exp(cums[i]) * carried
            for j in part_heads(half):
                cols = pl.ds(j * HD, HD)
                entering = jnp.dot(
                    lq[i, :, cols], incoming[i, cols, :], preferred_element_type=F32
                )
                mixed = inner[i, :, cols] + entering * reach[:, j:j + 1]
                mean_square = jnp.mean(mixed * mixed, axis=1, keepdims=True)
                source = 2 * group + j // 4
                gain = gains[source // 4, source % 4, pl.ds(j % 4, 1), :]
                lout[i, :, cols] = (mixed * lax.rsqrt(mean_square + 1e-6) * gain).astype(BF16)
            return carry

        lax.fori_loop(0, 2, finish, 0)
        cols = part_cols(half)
        target = lo_ref.at[:, part_cols(half, group * WIDE)]

        def send_out(d):
            other, device = zc(d)
            source = lout.at[other // 4, pl.ds((other % 4) * PIECE, PIECE), cols]
            push(LO[half], source, target, device)

        each(8, send_out)
        keep(LO[half], lout.at[c, rows, cols], target)

    def step(t, carry):
        def at(n, work, *args):
            pl.when(t == n)(lambda: work(*args))

        soft_piece(t)
        at(0, pass_on, 2)
        at(0, pass_gains)
        at(1, pass_on, 3)
        at(1, states, 0)
        at(1, send_near, 4)
        at(1, send_near, 5)
        at(3, states, 1)
        at(3, send_near, 6)
        at(3, pass_on, 4)
        at(3, entering_states, 0)
        at(3, send_near, 7)
        at(3, pass_on, 5)
        at(4, entering_states, 1)
        at(4, within, 0)
        at(4, pass_on, 6)
        at(4, light_outputs, 0)
        at(4, pass_on, 7)
        return carry

    send_near(0)
    lax.fori_loop(4, 6, send_z, 0)
    send_light(LK, 1, lk_ref, lk)
    send_light(LV, 1, lv_ref, lv)
    lax.fori_loop(6, 8, send_z, 0)
    send_light(LQ, 0, lq_ref, lq)
    send_light(LQ, 1, lq_ref, lq)
    send_near(1)
    pass_on(0)
    send_near(2)
    prepare()
    pass_on(1)
    send_near(3)
    all_queries()
    lax.fori_loop(0, 8, step, 0)
    within(1)
    light_outputs(1)

    landed(send.at[KV], kv.at[pl.ds(0, 7 * PIECE)])
    landed(send.at[DEC], dec_out.at[pl.ds(0, 7)])
    landed(send.at[GAIN], gains.at[0, pl.ds(0, 3)])
    landed(send.at[GAINS], gains.at[pl.ds(0, 3)])
    for kinds in (LK, LV, LQ, LO):
        for half in range(2):
            landed(send.at[kinds[half]], lk.at[:, pl.ds(0, 7 * 32), part_cols(half)])
    for kind in (SQ, SO):
        landed(send.at[kind], sq.at[pl.ds(0, 7)])
    landed(send.at[ZS], kv.at[pl.ds(0, 24 * PIECE)])
    landed(send.at[XS], kv.at[pl.ds(0, 24 * RUN)])
    landed(send.at[TOT], inner.at[0, pl.ds(0, 15 * 16), pl.ds(0, HD)])
    for half in range(2):
        for kind in (ST[half], IN[half]):
            landed(send.at[kind], kv.at[pl.ds(0, 15 * SLICE[half])])
        landed(recv.at[LO[half]], lo_ref.at[:, pl.ds(0, 8 * SPLIT[half][1] * HD)])
    landed(recv.at[SO], so_ref)


def per_device(
    light_query, light_key, light_value, light_decay, light_gain, soft_query, soft_kv, doc_blocks
):
    gain = light_gain.reshape(4, HD)
    anywhere = pl.BlockSpec(memory_space=pl.ANY)
    vmem = pl.BlockSpec(memory_space=pltpu.VMEM)
    out = jax.ShapeDtypeStruct((PIECE, 8 * WIDE), BF16)
    scratch = [
        pltpu.VMEM((2, RUN, WIDE), BF16),
        pltpu.VMEM((2, RUN, WIDE), BF16),
        pltpu.VMEM((2, RUN, WIDE), BF16),
        pltpu.VMEM((8, PIECE, 128), BF16),
        pltpu.VMEM((2, RUN, 128), BF16),
        pltpu.VMEM((4, 4, 8, HD), F32),
        pltpu.VMEM((2, RUN, WIDE), F32),
        pltpu.VMEM((2, RUN, WIDE), BF16),
        pltpu.VMEM((2, WIDE, HD), BF16),
        pltpu.VMEM((2, 8, 128), F32),
        pltpu.VMEM((4, 2, 4, SLICE[0], HD), BF16),
        pltpu.VMEM((4, 2, 4, SLICE[1], HD), BF16),
        pltpu.VMEM((4, 2, 4, 8, 128), F32),
        pltpu.VMEM((4, 2, 4, SLICE[0], HD), BF16),
        pltpu.VMEM((4, 2, 4, SLICE[1], HD), BF16),
        pltpu.VMEM((2, WIDE, HD), BF16),
        pltpu.VMEM((4, 2, 4, 8, 128), F32),
        pltpu.VMEM((8, PIECE, WIDE), BF16),
        pltpu.VMEM((9 * SHARD, 2 * HD), BF16),
        pltpu.VMEM((8, PIECE, 2 * HD), BF16),
        pltpu.VMEM((8, PIECE, WIDE), BF16),
        pltpu.VMEM((2, RUN, 128), F32),
        pltpu.VMEM((8, HD), F32),
        pltpu.VMEM((8 * ROWS, 2 * HD), BF16),
        pltpu.VMEM((9 * SHARD, HD), BF16),
        pltpu.VMEM((8 * ROWS, HD), F32),
        pltpu.VMEM((8 * ROWS, HD), F32),
        pltpu.VMEM((8 * ROWS, HD), F32),
        pltpu.SemaphoreType.DMA((KINDS,)),
        pltpu.SemaphoreType.DMA((KINDS,)),
        pltpu.SemaphoreType.DMA((8,)),
        pltpu.SemaphoreType.DMA((8,)),
        pltpu.SemaphoreType.DMA((8,)),
        pltpu.SemaphoreType.DMA((8,)),
        pltpu.SemaphoreType.DMA((8,)),
    ]
    return pl.pallas_call(
        kernel,
        out_shape=(out, out),
        in_specs=[
            pl.BlockSpec(memory_space=pltpu.SMEM), anywhere, anywhere, anywhere, vmem, vmem,
            anywhere, vmem,
        ],
        out_specs=(anywhere, anywhere),
        scratch_shapes=scratch,
        compiler_params=pltpu.CompilerParams(
            collective_id=0, has_side_effects=True, vmem_limit_bytes=63 * 2**20
        ),
    )(doc_blocks, light_query, light_key, light_value, light_decay, gain, soft_query, soft_kv)


def solution(mesh):
    placed = (
        P(("seq", "head"), None),
        P(("seq", "head"), None),
        P(("seq", "head"), None),
        P(("seq", "head"), None),
        P("head"),
        P(("seq", "head"), None),
        P(("seq", "head"), None, None),
        P(),
    )
    return jax.shard_map(
        per_device,
        mesh=mesh,
        in_specs=placed,
        out_specs=(P(("seq", "head"), None), P(("seq", "head"), None)),
        check_vma=False,
    )
```

```python
import functools
import itertools
import math

import jax
import jax.numpy as jnp
from jax import lax
from jax.experimental import pallas as pl
from jax.experimental.pallas import tpu as pltpu
from jax.sharding import PartitionSpec as P

MESH = pl.DeviceIdType.MESH
F32, BF16 = jnp.float32, jnp.bfloat16
HD = 128
RUN = 256
PIECE = 64
WIDE = 1024
SHARD = 1024
SPAN = 1024
ROWS = 8 * PIECE
LOG2E = math.log2(math.e)
SCALE = LOG2E / math.sqrt(HD)
NEG = -1e30

KV, DEC, GAIN, GAINS, SQ, TOT, SO, ZS, XS = range(9)
LK, LV, LQ, ST, IN, LO = ((9 + 2 * i, 10 + 2 * i) for i in range(6))
KINDS = 21
SPLIT = ((0, 6), (6, 2))
SLICE = (48, 16)

NT = (((1,), (1,)), ((), ()))
TN = (((0,), (0,)), ((), ()))


def kernel(
    docs_ref, lq_ref, lk_ref, lv_ref, dec_ref, gain_ref, sq_ref, kv_ref,
    lo_ref, so_ref,
    lq, lk, lv, dec_out, dec, gains, inner, lout, part, tot, parts0, parts1, tots, back0, back1, incoming, factors,
    sq, kv, kv_out, sout, cums, gain_out, queries, marks, top, denominator, acc, send, recv, kv_recv, z_recv, left_recv, right_recv, far_recv,
):
    s = lax.axis_index("seq")
    h = lax.axis_index("head")
    y, c = s // 2, s % 2
    x, z = h // 4, h % 4
    group = c * 4 + z
    member = y * 4 + x

    parts, back = (parts0, parts1), (back0, back1)

    def part_cols(half, start=0):
        first, heads = SPLIT[half]
        return pl.ds(start + first * HD, heads * HD)

    def part_heads(half):
        first, heads = SPLIT[half]
        return range(first, first + heads)

    def yc(d):
        return (s + d) % 8

    def zc(d):
        other = (group + d) % 8
        return other, (y * 2 + other // 4, x * 4 + other % 4)

    def along_x(d):
        return (s, ((x + d) % 4) * 4 + z)

    def along_z(d):
        return (s, x * 4 + (z + d) % 4)

    def xy(d):
        other = (member + d) % 16
        return other, ((other // 4) * 2 + c, (other % 4) * 4 + z)

    def push(kind, src, dst, device, recv_sem=None):
        pltpu.make_async_remote_copy(
            src_ref=src, dst_ref=dst, send_sem=send.at[kind],
            recv_sem=recv.at[kind] if recv_sem is None else recv_sem,
            device_id=device, device_id_type=MESH,
        ).start()

    def keep(kind, src, dst):
        pltpu.make_async_copy(src, dst, recv.at[kind]).start()

    def landed(sem, ref):
        pltpu.make_async_copy(ref, ref, sem).wait()

    def each(n, body):
        def step(d, carry):
            body(d)
            return carry
        lax.fori_loop(1, n, step, 0)

    barrier = pltpu.get_barrier_semaphore()

    def greet(device):
        pl.semaphore_signal(barrier, inc=1, device_id=device, device_id_type=MESH)

    each(8, lambda d: greet((yc(d), h)))
    each(8, lambda d: greet(zc(d)[1]))
    each(16, lambda d: greet(xy(d)[1]))
    gain = gain_ref[...].astype(F32)
    gain_out[...] = jnp.concatenate([gain, gain], axis=0)
    wide = jnp.concatenate([dec_ref[...], dec_ref[...]], axis=1).astype(F32)
    for g in range(8):
        dec_out[g] = (wide if g == 0 else pltpu.roll(wide, 128 - 8 * g, 1)).astype(BF16)
    for g in range(8):
        for i in range(2):
            kv_out[g, :, pl.ds(i * HD, HD)] = kv_ref[:, i, pl.ds(g * HD, HD)]
    pl.semaphore_wait(barrier, 7 + 7 + 15)

    mine = pl.ds(SHARD + s * SHARD + h * PIECE, PIECE)

    def send_kv(d):
        to = yc(d)
        push(KV, kv_out.at[to], kv.at[mine], (to, h), kv_recv.at[s])

    each(8, send_kv)
    pltpu.make_async_copy(kv_out.at[s], kv.at[mine], kv_recv.at[s]).start()

    rows = pl.ds(z * PIECE, PIECE)

    def send_light(kinds, half, ref, buf, some=None):
        first, heads = some or SPLIT[half]
        place = buf.at[c, rows, pl.ds(first * HD, heads * HD)]
        def one(d):
            other, device = zc(d)
            source = ref.at[:, pl.ds(other * WIDE + first * HD, heads * HD)]
            push(kinds[half], source, place, device)
        each(8, one)
        keep(kinds[half], ref.at[:, pl.ds(group * WIDE + first * HD, heads * HD)], place)

    def send_dec(d):
        other, device = zc(d)
        push(DEC, dec_out.at[other], dec.at[c, rows, :], device)

    send_light(LK, 0, lk_ref, lk, (0, 2))

    ends = []
    total = jnp.int32(0)
    for i in range(8):
        total = total + docs_ref[i] * 128
        ends.append(total)

    def doc_of(pos):
        found = jnp.zeros_like(pos)
        for end in ends:
            found = found + jnp.where(pos >= end, 1, 0)
        return found

    lane = lax.broadcasted_iota(jnp.int32, (1, HD), 1)
    doc_first = jnp.zeros((1, HD), jnp.int32)
    doc_end = jnp.zeros((1, HD), jnp.int32)
    for i, end in enumerate(ends):
        doc_first = jnp.where(lane == i, ends[i - 1] if i else 0, doc_first)
        doc_end = jnp.where(lane == i, end, doc_end)

    def mark(n, carry):
        at_row = pl.ds(pl.multiple_of(n * SHARD, SHARD), SHARD)
        row = lax.broadcasted_iota(jnp.int32, (SHARD, HD), 0)
        lanes = lax.broadcasted_iota(jnp.int32, (SHARD, HD), 1)
        token = (n - 1) * SHARD + row
        in_doc = (token >= doc_first) & (token < doc_end)
        own = (row == h * PIECE + lanes - 64) & (lanes >= 64)
        outside = (lanes == 8) & (token < 0)
        marks[at_row, :] = jnp.where(in_doc | own | outside, 1.0, 0.0).astype(BF16)
        return carry

    lax.fori_loop(0, 9, mark, 0)
    kv[pl.ds(0, SHARD), :] = jnp.zeros((SHARD, 2 * HD), BF16)


    def send_z(t, carry):
        landed(kv_recv.at[t], kv.at[pl.ds(0, PIECE)])
        block_rows = kv.at[pl.ds(SHARD + t * SHARD + h * PIECE, PIECE)]
        each(4, lambda d: push(ZS, block_rows, block_rows, along_z(d), z_recv.at[t]))
        return carry

    lax.fori_loop(0, 4, send_z, 0)
    def send_sq(d):
        to = yc(d)
        push(SQ, sq_ref.at[:, pl.ds(to * WIDE, WIDE)], sq.at[s], (to, h))

    each(8, send_sq)
    keep(SQ, sq_ref.at[:, pl.ds(s * WIDE, WIDE)], sq.at[s])

    each(8, send_dec)
    keep(DEC, dec_out.at[group], dec.at[c, rows, :])
    each(4, lambda d: push(GAIN, gain_out, gains.at[x, z], along_z(d)))
    keep(GAIN, gain_out, gains.at[x, z])
    send_light(LK, 0, lk_ref, lk, (2, 4))
    send_light(LV, 0, lv_ref, lv)
    def pass_gains():
        landed(recv.at[GAIN], gains.at[0])
        each(4, lambda d: push(GAINS, gains.at[x], gains.at[x], along_x(d)))


    def continues(p, carry):
        same = jnp.where(doc_of(p * RUN + RUN - 1) == doc_of(p * RUN - 1), 1.0, 0.0)
        factors[p // 8, (p // 4) % 2, p % 4] = jnp.full((8, 128), same, F32)
        return carry

    def prepare():
        lax.fori_loop(0, 32, continues, 0)
        top[...] = jnp.full_like(top, NEG)
        denominator[...] = jnp.zeros_like(denominator)
        acc[...] = jnp.zeros_like(acc)

    def send_near(t):
        landed(z_recv.at[t], kv.at[pl.ds(0, 3 * PIECE)])
        block_rows = kv.at[pl.ds(SHARD + t * SHARD + x * RUN, RUN)]
        push(XS, block_rows, block_rows, along_x(1), left_recv.at[t])
        push(XS, block_rows, block_rows, along_x(3), right_recv.at[t])

    def pass_on(t):
        landed(left_recv.at[t], kv.at[pl.ds(0, RUN)])
        landed(right_recv.at[t], kv.at[pl.ds(0, RUN)])
        way = 1 + 2 * (t % 2)
        block_rows = kv.at[pl.ds(SHARD + t * SHARD + ((x + 4 - way) % 4) * RUN, RUN)]
        push(XS, block_rows, block_rows, along_x(way), far_recv.at[t])

    column = lax.broadcasted_iota(jnp.int32, (RUN, 1), 0)
    line = lax.broadcasted_iota(jnp.int32, (1, RUN), 1)
    causal = column >= line
    lower = jnp.where(causal, 1.0, 0.0).astype(BF16)

    def run_start(i):
        return (2 * y + i) * SHARD + x * RUN

    def sum_decays(i, carry):
        cum = jnp.dot(lower, dec[i], preferred_element_type=F32)
        cums[i] = cum
        tot[i] = jnp.broadcast_to(cum.T[0:8, RUN - 1:RUN], (8, 128))
        return carry

    def slice_rows(half, owner):
        return pl.ds(SPLIT[half][0] * HD + owner * SLICE[half], SLICE[half])

    def states(half):
        if half == 0:
            landed(recv.at[DEC], dec)
            lax.fori_loop(0, 2, sum_decays, 0)
        landed(recv.at[LK[half]], lk.at[:, :, part_cols(half)])
        landed(recv.at[LV[half]], lv.at[:, :, part_cols(half)])

        def add_states(i, carry):
            cum = cums[i]
            start = run_start(i)
            last = doc_of(start + RUN - 1)
            tail = jnp.exp(cum[RUN - 1:RUN, :] - cum)
            tail = tail * jnp.where(doc_of(start + column) == last, 1.0, 0.0)
            for j in part_heads(half):
                cols = pl.ds(j * HD, HD)
                weighted = (lv[i, :, cols].astype(F32) * tail[:, j:j + 1]).astype(BF16)
                added = lax.dot_general(lk[i, :, cols], weighted, TN, preferred_element_type=F32)
                part[i, cols, :] = added.astype(BF16)
            return carry

        lax.fori_loop(0, 2, add_states, 0)

        def send_state(d):
            other, device = xy(d)
            if half == 0:
                push(TOT, tot, tots.at[y, :, x], device)
            mine = part.at[:, slice_rows(half, other), :]
            push(ST[half], mine, parts[half].at[y, :, x], device)

        each(16, send_state)
        if half == 0:
            keep(TOT, tot, tots.at[y, :, x])
        mine = part.at[:, slice_rows(half, member), :]
        keep(ST[half], mine, parts[half].at[y, :, x])

    def within(half):
        landed(recv.at[LQ[half]], lq.at[:, :, part_cols(half)])

        def inner_run(i, carry):
            cum = cums[i]
            across = cum.T
            start = run_start(i)
            allowed = causal & (doc_of(start + column) == doc_of(start + line))
            for j in part_heads(half):
                cols = pl.ds(j * HD, HD)
                gap = cum[:, j:j + 1] - across[j:j + 1, :]
                weight = jnp.exp(jnp.where(allowed, gap, NEG))
                scores = lax.dot_general(
                    lq[i, :, cols], lk[i, :, cols], NT, preferred_element_type=F32
                )
                inner[i, :, cols] = jnp.dot(
                    (scores * weight).astype(BF16), lv[i, :, cols], preferred_element_type=F32
                )
            return carry

        lax.fori_loop(0, 2, inner_run, 0)

    def entering_states(half):
        if half == 0:
            landed(recv.at[TOT], tots)
            factors[...] = factors[...] * jnp.exp(tots[...])
        landed(recv.at[ST[half]], parts[half])
        own_first = member * SLICE[half]
        head = own_first // HD
        after = jnp.minimum(head + 1, SPLIT[half][1] - 1)
        in_head = own_first + lax.broadcasted_iota(jnp.int32, (SLICE[half], HD), 0) < (head + 1) * HD

        state = jnp.zeros((SLICE[half], HD), F32)
        for a, b, e in itertools.product(range(4), range(2), range(4)):
            back[half][a, b, e] = state.astype(BF16)
            one = factors[a, b, e, pl.ds(SPLIT[half][0] + head, 1), :]
            two = factors[a, b, e, pl.ds(SPLIT[half][0] + after, 1), :]
            state = state * jnp.where(in_head, one, two) + parts[half][a, b, e].astype(F32)
        place = incoming.at[:, slice_rows(half, member), :]

        def send_back(d):
            other, device = xy(d)
            push(IN[half], back[half].at[other // 4, :, other % 4], place, device)

        each(16, send_back)
        keep(IN[half], back[half].at[y, :, x], place)

    def take_queries(t, carry):
        first = t * SHARD + h * PIECE
        inside = (first >= doc_first) & (first < doc_end)
        kept = jnp.where((lane > 8) | inside, 0.0, NEG).astype(BF16)
        for j in range(8):
            at_row = pl.ds(pl.multiple_of(t * ROWS, ROWS) + j * PIECE, PIECE)
            queries[at_row, pl.ds(0, HD)] = sq[t, :, pl.ds(j * HD, HD)]
            queries[at_row, pl.ds(HD, HD)] = jnp.broadcast_to(kept, (PIECE, HD))
        return carry

    def all_queries():
        landed(recv.at[SQ], sq)
        lax.fori_loop(0, 8, take_queries, 0)

    def key_block(t, count):
        first_row = pl.multiple_of(t * ROWS, ROWS)
        at_rows = pl.ds(first_row, count * ROWS)
        start = pl.multiple_of(t * SHARD + h * PIECE + PIECE, PIECE)
        keys = jnp.concatenate(
            [kv[pl.ds(start, SPAN), pl.ds(0, HD)], marks[pl.ds(start, SPAN), :]], axis=1
        )
        scores = lax.dot_general(queries[at_rows, :], keys, NT, preferred_element_type=F32)
        tiles = [scores[:, i * HD:(i + 1) * HD] for i in range(SPAN // HD)]
        highest = functools.reduce(jnp.maximum, tiles)
        old = top[at_rows, :]
        new = jnp.maximum(old, jnp.broadcast_to(jnp.max(highest, axis=1, keepdims=True), old.shape))
        top[at_rows, :] = new
        rescale = jnp.exp2((old - new) * SCALE)
        weights = [jnp.exp2((tile - new) * SCALE) for tile in tiles]
        denominator[at_rows, :] = functools.reduce(jnp.add, weights, denominator[at_rows, :] * rescale)
        rounded = jnp.concatenate([w.astype(BF16) for w in weights], axis=1)
        product = jnp.dot(rounded, kv[pl.ds(start, SPAN), pl.ds(HD, HD)], preferred_element_type=F32)
        acc[at_rows, :] = acc[at_rows, :] * rescale + product

    def soft_piece(t):
        landed(far_recv.at[t], kv.at[pl.ds(0, RUN)])
        at_rows = pl.ds(pl.multiple_of(t * ROWS, ROWS), ROWS)
        token = lax.broadcasted_iota(jnp.int32, (ROWS, HD), 0) % PIECE
        lanes = lax.broadcasted_iota(jnp.int32, (ROWS, HD), 1)
        kept = queries[at_rows, pl.ds(HD, HD)].astype(F32)
        queries[at_rows, pl.ds(HD, HD)] = jnp.where(lanes - 64 > token, NEG, kept).astype(BF16)
        pl.when(t <= 4)(lambda: key_block(t, 4))
        for last in (5, 6, 7):
            pl.when(t == last)(functools.partial(key_block, t, 8 - last))
        whole = jnp.sum(denominator[at_rows, :], axis=1, keepdims=True)
        result = (acc[at_rows, :] / whole).astype(BF16)
        for j in range(8):
            sout[t, :, pl.ds(j * HD, HD)] = result[j * PIECE:(j + 1) * PIECE, :]

        target = so_ref.at[:, pl.ds(s * WIDE, WIDE)]

        @pl.when(t == s)
        def _():
            keep(SO, sout.at[t], target)

        @pl.when(t != s)
        def _():
            push(SO, sout.at[t], target, (t, h))

    def light_outputs(half):
        if half == 0:
            landed(recv.at[GAINS], gains.at[pl.ds(0, 3)])
        landed(recv.at[IN[half]], incoming.at[:, part_cols(half), :])

        def finish(i, carry):
            start = run_start(i)
            carried = jnp.where(doc_of(start + column) == doc_of(start - 1), 1.0, 0.0)
            reach = jnp.exp(cums[i]) * carried
            for j in part_heads(half):
                cols = pl.ds(j * HD, HD)
                entering = jnp.dot(
                    lq[i, :, cols], incoming[i, cols, :], preferred_element_type=F32
                )
                mixed = inner[i, :, cols] + entering * reach[:, j:j + 1]
                mean_square = jnp.mean(mixed * mixed, axis=1, keepdims=True)
                source = 2 * group + j // 4
                gain = gains[source // 4, source % 4, pl.ds(j % 4, 1), :]
                lout[i, :, cols] = (mixed * lax.rsqrt(mean_square + 1e-6) * gain).astype(BF16)
            return carry

        lax.fori_loop(0, 2, finish, 0)
        cols = part_cols(half)
        target = lo_ref.at[:, part_cols(half, group * WIDE)]

        def send_out(d):
            other, device = zc(d)
            source = lout.at[other // 4, pl.ds((other % 4) * PIECE, PIECE), cols]
            push(LO[half], source, target, device)

        each(8, send_out)
        keep(LO[half], lout.at[c, rows, cols], target)

    def step(t, carry):
        def at(n, work, *args):
            pl.when(t == n)(lambda: work(*args))

        soft_piece(t)
        at(0, pass_on, 2)
        at(0, pass_gains)
        at(1, pass_on, 3)
        at(1, states, 0)
        at(1, send_near, 4)
        at(1, send_near, 5)
        at(3, states, 1)
        at(3, pass_on, 4)
        at(3, send_near, 6)
        at(3, entering_states, 0)
        at(3, send_near, 7)
        at(3, pass_on, 5)
        at(4, entering_states, 1)
        at(4, within, 0)
        at(4, pass_on, 6)
        at(4, light_outputs, 0)
        at(4, pass_on, 7)
        return carry

    send_near(0)
    lax.fori_loop(4, 6, send_z, 0)
    send_light(LK, 1, lk_ref, lk)
    send_light(LV, 1, lv_ref, lv)
    lax.fori_loop(6, 8, send_z, 0)
    send_light(LQ, 0, lq_ref, lq)
    send_light(LQ, 1, lq_ref, lq)
    send_near(1)
    pass_on(0)
    send_near(2)
    prepare()
    pass_on(1)
    send_near(3)
    all_queries()
    lax.fori_loop(0, 8, step, 0)
    within(1)
    light_outputs(1)

    landed(send.at[KV], kv.at[pl.ds(0, 7 * PIECE)])
    landed(send.at[DEC], dec_out.at[pl.ds(0, 7)])
    landed(send.at[GAIN], gains.at[0, pl.ds(0, 3)])
    landed(send.at[GAINS], gains.at[pl.ds(0, 3)])
    for kinds in (LK, LV, LQ, LO):
        for half in range(2):
            landed(send.at[kinds[half]], lk.at[:, pl.ds(0, 7 * 32), part_cols(half)])
    for kind in (SQ, SO):
        landed(send.at[kind], sq.at[pl.ds(0, 7)])
    landed(send.at[ZS], kv.at[pl.ds(0, 24 * PIECE)])
    landed(send.at[XS], kv.at[pl.ds(0, 24 * RUN)])
    landed(send.at[TOT], inner.at[0, pl.ds(0, 15 * 16), pl.ds(0, HD)])
    for half in range(2):
        for kind in (ST[half], IN[half]):
            landed(send.at[kind], kv.at[pl.ds(0, 15 * SLICE[half])])
        landed(recv.at[LO[half]], lo_ref.at[:, pl.ds(0, 8 * SPLIT[half][1] * HD)])
    landed(recv.at[SO], so_ref)


def per_device(
    light_query, light_key, light_value, light_decay, light_gain, soft_query, soft_kv, doc_blocks
):
    gain = light_gain.reshape(4, HD)
    anywhere = pl.BlockSpec(memory_space=pl.ANY)
    vmem = pl.BlockSpec(memory_space=pltpu.VMEM)
    out = jax.ShapeDtypeStruct((PIECE, 8 * WIDE), BF16)
    scratch = [
        pltpu.VMEM((2, RUN, WIDE), BF16),
        pltpu.VMEM((2, RUN, WIDE), BF16),
        pltpu.VMEM((2, RUN, WIDE), BF16),
        pltpu.VMEM((8, PIECE, 128), BF16),
        pltpu.VMEM((2, RUN, 128), BF16),
        pltpu.VMEM((4, 4, 8, HD), F32),
        pltpu.VMEM((2, RUN, WIDE), F32),
        pltpu.VMEM((2, RUN, WIDE), BF16),
        pltpu.VMEM((2, WIDE, HD), BF16),
        pltpu.VMEM((2, 8, 128), F32),
        pltpu.VMEM((4, 2, 4, SLICE[0], HD), BF16),
        pltpu.VMEM((4, 2, 4, SLICE[1], HD), BF16),
        pltpu.VMEM((4, 2, 4, 8, 128), F32),
        pltpu.VMEM((4, 2, 4, SLICE[0], HD), BF16),
        pltpu.VMEM((4, 2, 4, SLICE[1], HD), BF16),
        pltpu.VMEM((2, WIDE, HD), BF16),
        pltpu.VMEM((4, 2, 4, 8, 128), F32),
        pltpu.VMEM((8, PIECE, WIDE), BF16),
        pltpu.VMEM((9 * SHARD, 2 * HD), BF16),
        pltpu.VMEM((8, PIECE, 2 * HD), BF16),
        pltpu.VMEM((8, PIECE, WIDE), BF16),
        pltpu.VMEM((2, RUN, 128), F32),
        pltpu.VMEM((8, HD), F32),
        pltpu.VMEM((8 * ROWS, 2 * HD), BF16),
        pltpu.VMEM((9 * SHARD, HD), BF16),
        pltpu.VMEM((8 * ROWS, HD), F32),
        pltpu.VMEM((8 * ROWS, HD), F32),
        pltpu.VMEM((8 * ROWS, HD), F32),
        pltpu.SemaphoreType.DMA((KINDS,)),
        pltpu.SemaphoreType.DMA((KINDS,)),
        pltpu.SemaphoreType.DMA((8,)),
        pltpu.SemaphoreType.DMA((8,)),
        pltpu.SemaphoreType.DMA((8,)),
        pltpu.SemaphoreType.DMA((8,)),
        pltpu.SemaphoreType.DMA((8,)),
    ]
    return pl.pallas_call(
        kernel,
        out_shape=(out, out),
        in_specs=[
            pl.BlockSpec(memory_space=pltpu.SMEM), anywhere, anywhere, anywhere, vmem, vmem,
            anywhere, vmem,
        ],
        out_specs=(anywhere, anywhere),
        scratch_shapes=scratch,
        compiler_params=pltpu.CompilerParams(
            collective_id=0, has_side_effects=True, vmem_limit_bytes=63 * 2**20
        ),
    )(doc_blocks, light_query, light_key, light_value, light_decay, gain, soft_query, soft_kv)


def solution(mesh):
    placed = (
        P(("seq", "head"), None),
        P(("seq", "head"), None),
        P(("seq", "head"), None),
        P(("seq", "head"), None),
        P("head"),
        P(("seq", "head"), None),
        P(("seq", "head"), None, None),
        P(),
    )
    return jax.shard_map(
        per_device,
        mesh=mesh,
        in_specs=placed,
        out_specs=(P(("seq", "head"), None), P(("seq", "head"), None)),
        check_vma=False,
    )
```
